32 devices in a mesh: seq: 8 (over z, y), rep: 2 (over x), own: 2 (over core).
Axes of the slice: x: 2, y: 2, z: 4, core: 2. Of those that a mesh axis runs over, the one named last changes fastest.
Arguments:
- latent: bfloat16 [4096, 8, 1280], P('seq', ('rep', 'own')), may hold values from -40 to 40
- cotangent: bfloat16 [4096, 8, 1280], P('seq', ('rep', 'own')), may hold values from -16 to 16
- norm_gain: float32 [1280], replicated, may hold values from 0.1 to 1.9
- norm_shift: float32 [1280], replicated, may hold values from -3 to 3
- proj_qkv: bfloat16 [1280, 3072], P('own'), may hold values from -1 to 1
- proj_out: bfloat16 [1024, 1280], P('own'), may hold values from -0.1875 to 0.1875
Outputs:
- mixed: bfloat16 [4096, 8, 1280], P('seq', ('rep', 'own'))
- grad_latent: bfloat16 [4096, 8, 1280], P('seq', ('rep', 'own'))
- grad_proj_qkv: float32 [1280, 3072], P(('seq', 'rep', 'own'))
- grad_proj_out: float32 [1024, 1280], P(('seq', 'rep', 'own'))
The draws below stay inside these ranges and needn't reach their ends.
All inputs are finite; a program needn't handle non-finite values.
Results may differ from the reference program's by a relative error of at most 0.0055.
The reference program's roundings to bfloat16 on the way (of `normed`, `projected`, `probs_low`, `attended`, `grad_attended`, `dscores` and `grad_projected`) count: a program that leaves them out, or rounds other values in their place, can miss the bound.
Values may be sent and summed in bfloat16 or wider, within the bound.
No kernel may reach another device: no remote copies, remote signals or barrier semaphores. Data moves between devices by JAX's collectives and lax.ppermute only.
A program may use at most 192 MiB of HBM per device.

```python
import math
import jax
import jax.numpy as jnp
from jax import lax

C = 1280
HEADS = 16
HEAD = 64
GROUPS = 32
L = 4096
BATCH = 8


def draw_latent(key, part):
    key_row, key_col, key_base = jax.random.split(key, 3)
    position = jnp.arange(L, dtype=jnp.float32) / L
    row_scale = 0.35 * jnp.exp(math.log(3.0) * position + jax.random.uniform(key_row, (L,), minval=-0.6, maxval=0.6))
    col_scale = jnp.exp(jax.random.uniform(key_col, (C,), minval=math.log(0.3), maxval=math.log(3.0)))
    values = jax.random.normal(key_base, (L, BATCH, C)) * row_scale[:, None, None] * col_scale[None, None, :]
    return jnp.clip(values, -40.0, 40.0).astype(jnp.bfloat16)


def draw_cotangent(key, part):
    key_row, key_base, key_common = jax.random.split(jax.random.fold_in(key, 7), 3)
    position = jnp.arange(L, dtype=jnp.float32) / L
    jitter = jax.random.uniform(key_row, (L,), minval=-0.3, maxval=0.3)
    row_scale = 0.5 * jnp.exp(math.log(3.0) * position + jitter)
    base = jax.random.normal(key_base, (L, BATCH, C))
    common = 1.2 * jax.random.normal(key_common, (1, BATCH, C))
    values = (base + common) * row_scale[:, None, None]
    return jnp.clip(values, -16.0, 16.0).astype(jnp.bfloat16)


def draw_proj_qkv(key, part):
    key_query, key_key, key_value = jax.random.split(key, 3)
    inner_width = HEADS * HEAD
    sharp = 1.6 / math.sqrt(C)
    drawn = 1.0 / math.sqrt(C)
    query_part = jax.random.normal(key_query, (C, inner_width)) * sharp
    key_part = jax.random.normal(key_key, (C, inner_width)) * sharp
    value_part = jax.random.normal(key_value, (C, inner_width)) * drawn
    return jnp.clip(jnp.concatenate([query_part, key_part, value_part], axis=1), -1.0, 1.0).astype(jnp.bfloat16)


def levels(stream_key, extent, cuts, least, top_value):
    loudness, own = 1.0, jax.random.fold_in(stream_key, 6)
    for dim, blocks in cuts:
        steps = jnp.exp(jax.random.uniform(jax.random.fold_in(own, dim), (blocks,), jnp.float32, least / len(cuts), top_value / len(cuts)))
        loudness = loudness * jnp.repeat(steps, extent[dim] // blocks).reshape([-1 if axis == dim else 1 for axis in range(len(extent))])
    return loudness


def bell_draw(rng, dims, width, limit, shards=(), kind=jnp.bfloat16):
    values = jax.random.normal(rng, dims, jnp.float32) * width
    if len(shards) > 0:
        values = levels(rng, dims, shards, -0.22, 0.18) * values
    return jnp.clip(values, min=-limit, max=limit).astype(kind)


def setup_inputs(seed: int = 0) -> dict:
    keys = jax.random.split(jax.random.key(seed), 7)
    return {
        "latent": draw_latent(jax.random.fold_in(keys[6], 71), 0),
        "cotangent": draw_cotangent(jax.random.fold_in(keys[6], 71), 0),
        "norm_gain": jnp.clip(1.0 + 0.18 * jax.random.normal(keys[2], (C,), jnp.float32), 0.1, 1.9),
        "norm_shift": bell_draw(keys[3], (C,), 0.5, 3.0, (), jnp.float32),
        "proj_qkv": draw_proj_qkv(jax.random.fold_in(keys[6], 71), 0),
        "proj_out": bell_draw(keys[5], (HEADS * HEAD, C), (HEADS * HEAD) ** -0.5, 0.1875, ((0, 2),)),
    }


def reference(latent, cotangent, norm_gain, norm_shift, proj_qkv, proj_out):
    length, images, channels = latent.shape
    per_group = channels // GROUPS
    inner_width = HEADS * HEAD
    score_scale = HEAD ** (-0.5)
    total_count = length * per_group
    values = latent.astype(jnp.float32)
    grouped = values.reshape(length, images, GROUPS, per_group)
    group_mean = lax.optimization_barrier(jnp.sum(grouped, axis=(0, 3))) / total_count
    group_meansq = lax.optimization_barrier(jnp.sum(grouped * grouped, axis=(0, 3))) / total_count
    inv_std = lax.rsqrt(group_meansq - group_mean * group_mean + 1e-06)
    centred = (grouped - group_mean[None, :, :, None]) * inv_std[None, :, :, None]
    normed = (centred.reshape(length, images, channels) * norm_gain + norm_shift).astype(jnp.bfloat16)
    normed_rows = normed.reshape(length * images, channels)
    projected = jnp.dot(normed_rows, proj_qkv, preferred_element_type=jnp.float32).astype(jnp.bfloat16)
    projected = projected.reshape(length, images, 3, HEADS, HEAD)
    grad_rows = cotangent.reshape(length * images, channels)
    grad_attended = jnp.dot(grad_rows, proj_out.T, preferred_element_type=jnp.float32).astype(jnp.bfloat16)
    grad_attended = grad_attended.reshape(length, images, HEADS, HEAD)

    def to_pairs(array):
        return array.transpose(1, 2, 0, 3).reshape(images * HEADS, length, HEAD)

    def from_pairs(array):
        return array.reshape(images, HEADS, length, HEAD).transpose(2, 0, 1, 3).reshape(length * images, inner_width)

    def one_pair(operands):
        query, key_rows, value_rows, grad_block = operands
        scores = jnp.dot(query, key_rows.T, preferred_element_type=jnp.float32) * score_scale
        row_max = lax.optimization_barrier(jnp.max(scores, axis=-1, keepdims=True))
        weights = jnp.exp(scores - row_max)
        probs = weights / lax.optimization_barrier(jnp.sum(weights, axis=-1, keepdims=True))
        probs_low = probs.astype(jnp.bfloat16)
        attended = jnp.dot(probs_low, value_rows, preferred_element_type=jnp.float32).astype(jnp.bfloat16)
        dprobs = jnp.dot(grad_block, value_rows.T, preferred_element_type=jnp.float32)
        row_delta = lax.optimization_barrier(jnp.sum(probs * dprobs, axis=-1, keepdims=True))
        dscores = (probs * (dprobs - row_delta) * score_scale).astype(jnp.bfloat16)
        grad_query = jnp.dot(dscores, key_rows, preferred_element_type=jnp.float32).astype(jnp.bfloat16)
        grad_key = jnp.dot(dscores.T, query, preferred_element_type=jnp.float32).astype(jnp.bfloat16)
        grad_value = jnp.dot(probs_low.T, grad_block, preferred_element_type=jnp.float32).astype(jnp.bfloat16)
        return (attended, grad_query, grad_key, grad_value)
    results = lax.map(one_pair, (to_pairs(projected[:, :, 0]), to_pairs(projected[:, :, 1]), to_pairs(projected[:, :, 2]), to_pairs(grad_attended)))
    attended_rows = from_pairs(results[0])
    mixed = (values + jnp.dot(attended_rows, proj_out, preferred_element_type=jnp.float32).reshape(length, images, channels)).astype(jnp.bfloat16)
    grad_proj_out = jnp.dot(attended_rows.T, grad_rows, preferred_element_type=jnp.float32)
    grad_projected = jnp.stack([from_pairs(results[1]).reshape(length, images, inner_width), from_pairs(results[2]).reshape(length, images, inner_width), from_pairs(results[3]).reshape(length, images, inner_width)], axis=2)
    grad_projected = grad_projected.reshape(length * images, 3 * inner_width)
    grad_proj_qkv = jnp.dot(normed_rows.T, grad_projected, preferred_element_type=jnp.float32)
    grad_normed = jnp.dot(grad_projected, proj_qkv.T, preferred_element_type=jnp.float32)
    grad_centred = (grad_normed.reshape(length, images, channels) * norm_gain).reshape(length, images, GROUPS, per_group)
    mean_one = lax.optimization_barrier(jnp.sum(grad_centred, axis=(0, 3))) / total_count
    mean_two = lax.optimization_barrier(jnp.sum(grad_centred * centred, axis=(0, 3))) / total_count
    grad_values = inv_std[None, :, :, None] * (grad_centred - mean_one[None, :, :, None] - centred * mean_two[None, :, :, None])
    grad_latent = (cotangent.astype(jnp.float32) + grad_values.reshape(length, images, channels)).astype(jnp.bfloat16)
    return (mixed, grad_latent, grad_proj_qkv, grad_proj_out)
```

```python
import functools
import math
import jax
import jax.numpy as jnp
from jax import lax
from jax.experimental import pallas as pl
from jax.experimental.pallas import tpu as pltpu
from jax.sharding import PartitionSpec as P

HEADS = 16
HEAD = 64
GROUPS = 32
EPS = 1e-06
LOG2E = math.log2(math.e)
PACK = 4 * HEAD
HALF = 2 * HEAD
ALL = ("seq", "rep", "own")
NT = (((1,), (1,)), ((), ()))
NN = (((1,), (0,)), ((), ()))
VMEM = 56 * 2**20


def dot(left, right, dims=NN):
    return lax.dot_general(left, right, dims, preferred_element_type=jnp.float32)


def low(array):
    return array.astype(jnp.bfloat16)


def eight_rows(array, op):
    return op(array.reshape(array.shape[0] // 8, 8, array.shape[1]), axis=0)


def pair_body(bq, kb, me_ref, *refs):
    ins, (o_ref, x_ref, kv_t, s_buf, dp_buf, acc, done) = refs[:-7], refs[-7:]
    length = x_ref.shape[0]
    piece = length // len(ins)
    for j, ref in enumerate(ins):
        x_ref[j * piece : (j + 1) * piece, :] = ref[...].reshape(piece, PACK)
    key_blocks, query_blocks = length // kb, length // bq
    step_len = min(512, length)
    first = lax.broadcasted_iota(jnp.int32, (1, HALF), 1) < HEAD
    zero = jnp.bfloat16(0)

    def prepare(j, carry):
        rows = pl.ds(pl.multiple_of(j * step_len, step_len), step_len)
        kv_t[:, rows] = low(x_ref[rows, 0:HALF].astype(jnp.float32).T)
        acc[rows, :] = jnp.zeros((step_len, HALF), jnp.float32)
        return carry

    lax.fori_loop(0, length // step_len, prepare, 0)

    def query_block(i):
        pair = x_ref[pl.ds(pl.multiple_of(i * bq, bq), bq), HALF:PACK]
        query = jnp.where(first, pair, zero) * jnp.bfloat16(HEAD**-0.5)
        return query, jnp.where(first, zero, pair)

    def score_block(j, query, buf, top):
        keys = slice(j * kb, (j + 1) * kb)
        scores = dot(x_ref[keys, 0:HALF], query, NT)
        s_buf[buf, keys, :] = scores
        return jnp.maximum(top, eight_rows(scores, jnp.max))

    def finish_top(top):
        return jnp.max(top, axis=0, keepdims=True) * LOG2E

    no_top = jnp.full((8, bq), -jnp.inf, jnp.float32)

    def step(i, top):
        buf = lax.rem(i, 2)
        query, grad = query_block(i)
        next_query, _ = query_block(lax.rem(i + 1, query_blocks))
        total = jnp.zeros((8, bq), jnp.float32)
        delta = jnp.zeros((8, bq), jnp.float32)
        for j in range(key_blocks):
            keys = slice(j * kb, (j + 1) * kb)
            dprobs = dot(x_ref[keys, 0:HALF], grad, NT)
            weights = jnp.exp2(s_buf[buf, keys, :] * LOG2E - top)
            s_buf[buf, keys, :] = weights
            dp_buf[keys, :] = dprobs
            total = total + eight_rows(weights, jnp.sum)
            delta = delta + eight_rows(weights * dprobs, jnp.sum)
        inverse = 1.0 / jnp.sum(total, axis=0, keepdims=True)
        delta = jnp.sum(delta, axis=0, keepdims=True) * inverse
        attended = jnp.zeros((HEAD, bq), jnp.float32)
        grad_query = jnp.zeros((HEAD, bq), jnp.float32)
        next_top = no_top
        for j in range(key_blocks):
            keys = slice(j * kb, (j + 1) * kb)
            probs = s_buf[buf, keys, :] * inverse
            probs_low = low(probs)
            dscores = low(probs * (dp_buf[keys, :] - delta))
            attended = attended + dot(kv_t[HEAD:HALF, keys], probs_low)
            grad_query = grad_query + dot(kv_t[0:HEAD, keys], dscores)
            acc[keys, :] += dot(dscores, query) + dot(probs_low, grad)
            next_top = score_block(j, next_query, 1 - buf, next_top)
        both = jnp.concatenate([grad_query * HEAD**-0.5, attended], axis=0)
        done[pl.ds(pl.multiple_of(i * bq, bq), bq), :] = low(both.T)
        return finish_top(next_top)

    top = no_top
    first_query, _ = query_block(0)
    for j in range(key_blocks):
        top = score_block(j, first_query, 0, top)
    lax.fori_loop(0, query_blocks, step, finish_top(top))

    tokens = o_ref.shape[1]
    for j in range(len(ins)):
        for half in range(2):
            rows = slice((2 * j + half) * tokens, (2 * j + half + 1) * tokens)
            owner = me_ref[0] ^ (half * len(ins) + j)
            o_ref[owner, :, 0:HALF] = low(acc[rows, :])
            o_ref[owner, :, HALF:PACK] = done[rows, :]


def attend_pair(pieces, me):
    tokens = pieces[0].shape[1]
    blocks = 2 * len(pieces)
    length = blocks * tokens
    bq, kb = min(256, length), min(256, length)
    vmem = pl.BlockSpec(memory_space=pltpu.VMEM)
    return pl.pallas_call(
        functools.partial(pair_body, bq, kb),
        out_shape=jax.ShapeDtypeStruct((blocks, tokens, PACK), jnp.bfloat16),
        in_specs=[pl.BlockSpec(memory_space=pltpu.SMEM)] + [vmem] * len(pieces),
        out_specs=vmem,
        scratch_shapes=[
            pltpu.VMEM((length, PACK), jnp.bfloat16),
            pltpu.VMEM((HALF, length), jnp.bfloat16),
            pltpu.VMEM((2, length, bq), jnp.float32),
            pltpu.VMEM((length, bq), jnp.float32),
            pltpu.VMEM((length, HALF), jnp.float32),
            pltpu.VMEM((length, HALF), jnp.bfloat16),
        ],
        compiler_params=pltpu.CompilerParams(vmem_limit_bytes=VMEM),
        cost_estimate=pl.CostEstimate(
            flops=6 * 2 * length * length * 256, bytes_accessed=4 * length * PACK, transcendentals=length * length
        ),
        name="attend_pair",
    )(me, *pieces)


def lane_piece(array, head, slot):
    piece = array[:, head * HEAD // HALF * HALF :][:, :HALF]
    return piece if head % 2 == slot % 2 else pltpu.roll(piece, HEAD, 1)


def project_body(count, groups, me_ref, norm_ref, grad_ref, wq_ref, wk_ref, wv_ref, *outs):
    first = lax.broadcasted_iota(jnp.int32, (1, HALF), 1) < HEAD
    width = count * HEAD
    weights = jnp.concatenate([wq_ref[...], wk_ref[...], wv_ref[...]], axis=1)
    projected = dot(norm_ref[0], weights)
    query, key, value = (projected[:, part * width : (part + 1) * width] for part in range(3))
    grad = grad_ref[0].astype(jnp.float32)
    packs = []
    for head in range(count):
        left = jnp.where(first, lane_piece(key, head, 0), lane_piece(value, head, 1))
        right = jnp.where(first, lane_piece(query, head, 0), lane_piece(grad, head, 1))
        packs.append(low(jnp.concatenate([left, right], axis=1)))
    for flip in range(groups):

        @pl.when(pl.program_id(1) == flip)
        def _():
            for head in range(count):
                outs[head * groups + flip][0] = packs[head]


def project(normed, grads, full_qkv, unit, heads, offset, count):
    halves, tokens, channels = normed.shape
    groups = HEADS // heads
    width = count * HEAD
    steps = heads // count
    rows = pl.BlockSpec((1, tokens, channels), lambda i, j, unit: (i, 0, 0))

    def columns(part):
        return pl.BlockSpec(
            (channels, width), lambda i, j, unit: (0, (part * groups + (j ^ unit[0])) * steps + offset // count)
        )

    results = pl.pallas_call(
        functools.partial(project_body, count, groups),
        out_shape=[jax.ShapeDtypeStruct((halves, tokens, PACK), jnp.bfloat16)] * (count * groups),
        grid_spec=pltpu.PrefetchScalarGridSpec(
            num_scalar_prefetch=1,
            grid=(halves, groups),
            in_specs=[
                rows,
                pl.BlockSpec((1, tokens, width), lambda i, j, unit: (i, 0, j ^ unit[0])),
                columns(0),
                columns(1),
                columns(2),
            ],
            out_specs=[pl.BlockSpec((1, tokens, PACK), lambda i, j, unit: (i, 0, 0))] * (count * groups),
        ),
        compiler_params=pltpu.CompilerParams(vmem_limit_bytes=VMEM),
        cost_estimate=pl.CostEstimate(
            flops=2 * halves * tokens * channels * 4 * groups * width, bytes_accessed=2**24, transcendentals=0
        ),
        name="project",
    )(unit, normed, grads, full_qkv, full_qkv, full_qkv)
    return [results[head * groups : (head + 1) * groups] for head in range(count)]


def project_plain(normed, grads, full_qkv, unit, heads, offset, count):
    halves, tokens, channels = normed.shape
    groups = HEADS // heads
    qkv = low(jnp.einsum("itc,cd->itd", normed, full_qkv, preferred_element_type=jnp.float32))
    split = qkv.reshape(halves, tokens, 3, groups, heads, HEAD)[:, :, :, :, offset : offset + count]
    grads = grads.reshape(halves, tokens, 1, groups, count, HEAD)
    packed = jnp.concatenate([split[:, :, 1:3], split[:, :, 0:1], grads], axis=2)
    packed = packed.transpose(4, 3, 0, 1, 2, 5).reshape(count, groups, halves, tokens, PACK)
    packed = jnp.take(packed, jnp.arange(groups) ^ unit[0], axis=1)
    return [[packed[head, flip] for flip in range(groups)] for head in range(count)]


def weight_body(images, norm_ref, cot_ref, *refs):
    grad_refs, o_ref = refs[:images], refs[images]
    grads = jnp.concatenate([ref[0] for ref in grad_refs], axis=0)
    split = lax.broadcasted_iota(jnp.int32, (1, PACK), 1) < 3 * HEAD
    zero = jnp.bfloat16(0)
    o_ref[...] = dot(norm_ref[...], jnp.where(split, grads, zero)) + dot(cot_ref[...], jnp.where(split, zero, grads))


def weight_grads(normed_t, cotangent_t, grads, images):
    channels, rows = normed_t.shape
    groups = grads.shape[0] // images
    tokens = grads.shape[1]
    whole = pl.BlockSpec((channels, rows), lambda g: (0, 0))

    def block(image):
        return pl.BlockSpec((1, tokens, PACK), lambda g: (image * groups + g, 0, 0))

    return pl.pallas_call(
        functools.partial(weight_body, images),
        out_shape=jax.ShapeDtypeStruct((channels, groups * PACK), jnp.float32),
        grid=(groups,),
        in_specs=[whole, whole] + [block(image) for image in range(images)],
        out_specs=pl.BlockSpec((channels, PACK), lambda g: (0, g)),
        compiler_params=pltpu.CompilerParams(vmem_limit_bytes=VMEM),
        cost_estimate=pl.CostEstimate(
            flops=4 * channels * rows * groups * PACK, bytes_accessed=2**23, transcendentals=0
        ),
        name="weight_grads",
    )(normed_t, cotangent_t, *([grads] * images))


def gather_heads(parts, slot):
    first = lax.broadcasted_iota(jnp.int32, (1, HALF), 1) < HEAD
    base = slot // 2 * HALF
    pieces = []
    for even in range(0, len(parts), 2):
        left, right = parts[even][:, base : base + HALF], parts[even + 1][:, base : base + HALF]
        if slot % 2 == 0:
            right = pltpu.roll(right, HEAD, 1)
        else:
            left = pltpu.roll(left, HEAD, 1)
        pieces.append(jnp.where(first, left, right))
    return low(jnp.concatenate(pieces, axis=1))


def back_body(heads, *refs):
    grads, (wq_ref, wk_ref, wv_ref, wo_ref, mix_ref, norm_ref) = refs[:heads], refs[heads:]
    g = pl.program_id(1)
    parts = [ref[0].astype(jnp.float32) for ref in grads]
    back = (
        dot(gather_heads(parts, 2), wq_ref[...], NT)
        + dot(gather_heads(parts, 0), wk_ref[...], NT)
        + dot(gather_heads(parts, 1), wv_ref[...], NT)
    )
    mixed = dot(gather_heads(parts, 3), wo_ref[...])

    @pl.when(g == 0)
    def _():
        norm_ref[0] = back
        mix_ref[0] = mixed

    @pl.when(g > 0)
    def _():
        norm_ref[0] += back
        mix_ref[0] += mixed


def project_back(grads, full_qkv, full_out, images):
    heads = len(grads)
    groups = HEADS // heads
    tokens = grads[0].shape[1]
    channels = full_qkv.shape[0]
    width = heads * HEAD

    def columns(part):
        return pl.BlockSpec((channels, width), lambda i, g: (0, part * groups + g))

    rows = pl.BlockSpec((1, tokens, channels), lambda i, g: (i, 0, 0))
    block = pl.BlockSpec((1, tokens, PACK), lambda i, g: (i * groups + g, 0, 0))
    return pl.pallas_call(
        functools.partial(back_body, heads),
        out_shape=[jax.ShapeDtypeStruct((images, tokens, channels), jnp.float32)] * 2,
        grid=(images, groups),
        in_specs=[block] * heads
        + [columns(0), columns(1), columns(2), pl.BlockSpec((width, channels), lambda i, g: (g, 0))],
        out_specs=[rows, rows],
        compiler_params=pltpu.CompilerParams(vmem_limit_bytes=VMEM),
        cost_estimate=pl.CostEstimate(
            flops=2 * images * tokens * channels * 4 * HEADS * HEAD, bytes_accessed=2**25, transcendentals=0
        ),
        name="project_back",
    )(*grads, full_qkv, full_qkv, full_qkv, full_out)


def project_back_plain(grads, full_qkv, full_out, images):
    heads = len(grads)
    groups = HEADS // heads
    tokens = grads[0].shape[1]
    packed = jnp.stack(grads).reshape(heads, images, groups, tokens, 4, HEAD)
    packed = packed.transpose(1, 3, 4, 2, 0, 5).reshape(images, tokens, 4, HEADS * HEAD)
    key, value, query, attended = (packed[:, :, slot] for slot in range(4))
    stacked = jnp.concatenate([query, key, value], axis=2)
    mixed = jnp.einsum("itd,dc->itc", attended, full_out, preferred_element_type=jnp.float32)
    back = jnp.einsum("itd,cd->itc", stacked, full_qkv, preferred_element_type=jnp.float32)
    return mixed, back


def flipped(array, axis, flip):
    return lax.ppermute(array, axis, [(i, i ^ flip) for i in range(lax.axis_size(axis))])


def sum_near(partial, seq_count):
    rep, own = lax.axis_size("rep"), lax.axis_size("own")
    columns = partial.shape[1]
    cut = partial.reshape(seq_count, rep * own, -1, columns)
    here = lax.axis_index("rep") * own + lax.axis_index("own")
    total = lax.dynamic_index_in_dim(cut, here, 1, keepdims=False)
    for flip in range(1, rep * own):
        sent = low(lax.dynamic_index_in_dim(cut, here ^ flip, 1, keepdims=False))
        total = total + flipped(sent, ("rep", "own"), flip).astype(jnp.float32)
    return low(total)


def sum_far(near):
    pieces = lax.all_to_all(near, "seq", split_axis=0, concat_axis=0, tiled=True)
    return jnp.sum(pieces.astype(jnp.float32), axis=0)


def shards(latent, cotangent, norm_gain, norm_shift, proj_qkv, proj_out):
    tokens, images, channels = latent.shape
    seq_count = lax.axis_size("seq")
    devices = seq_count * lax.axis_size("rep") * lax.axis_size("own")
    per_group = channels // GROUPS
    total_count = tokens * seq_count * per_group
    groups = seq_count // images
    heads = HEADS // groups
    aligned = heads * HEAD % HALF == 0

    full_qkv = lax.all_gather(proj_qkv, "own", axis=0, tiled=True)
    full_out = lax.all_gather(proj_out, "own", axis=0, tiled=True)

    def group_sums(*arrays):
        sums = jnp.stack([jnp.sum(a, axis=1).reshape(images, GROUPS, per_group).sum(axis=2) for a in arrays])
        return lax.psum(sums, "seq") / total_count

    def spread(array):
        return jnp.repeat(array, per_group, axis=1)[:, None, :]

    me = lax.axis_index("seq").astype(jnp.int32).reshape(1)
    unit = me % groups
    image = lax.axis_index("seq") // groups

    def pick(array, index):
        return lax.dynamic_index_in_dim(array, index, 0, keepdims=False)

    def swapped(array):
        return jnp.stack([pick(array, image), flipped(pick(array, 1 - image), "seq", groups)])

    rows = latent.transpose(1, 0, 2)
    cot_rows = cotangent.transpose(1, 0, 2)
    work = swapped(rows).astype(jnp.float32)
    count = 2 if aligned else heads
    offsets = range(0, heads, count)
    grad_parts = []
    for offset in offsets:
        part = full_out.reshape(groups, heads, HEAD, channels)[:, offset : offset + count]
        part = part.reshape(groups * count * HEAD, channels)
        grad_parts.append(swapped(low(jnp.einsum("itc,dc->itd", cot_rows, part, preferred_element_type=jnp.float32))))

    values = rows.astype(jnp.float32)
    group_mean, group_meansq = group_sums(values, values * values)
    group_inv = lax.rsqrt(group_meansq - group_mean * group_mean + EPS)
    mean, inv_std = spread(group_mean), spread(group_inv)
    centred = (values - mean) * inv_std
    normed = low(centred * norm_gain + norm_shift)
    normed_t = normed.reshape(images * tokens, channels).T
    cotangent_t = cot_rows.reshape(images * tokens, channels).T
    work_normed = low((work - pick(mean, image)) * pick(inv_std, image) * norm_gain + norm_shift)

    sends = []
    for offset, part in zip(offsets, grad_parts):
        sends += (project if aligned else project_plain)(work_normed, part, full_qkv, unit, heads, offset, count)
    grads, nears = [], []
    result = None
    for head in range(heads):
        pieces = [sends[head][0]] + [flipped(sends[head][flip], "seq", flip) for flip in range(1, groups)]
        if head == 0:
            pieces, normed_t, cotangent_t = lax.optimization_barrier((pieces, normed_t, cotangent_t))
        if head >= 1:
            pieces, result = lax.optimization_barrier((pieces, result))
            grads.append(lax.all_to_all(result, "seq", split_axis=0, concat_axis=0, tiled=True))
        if head + 1 < heads:
            pieces, sends[head + 1] = lax.optimization_barrier((pieces, sends[head + 1]))
        if head >= 2:
            partial = weight_grads(normed_t, cotangent_t, grads[head - 2], images)
            pieces, partial, grads[head - 2] = lax.optimization_barrier((pieces, partial, grads[head - 2]))
            nears.append(sum_near(partial, seq_count))
        if head >= 3:
            pieces, nears[head - 3] = lax.optimization_barrier((pieces, nears[head - 3]))
        result = attend_pair(pieces, me)
    if heads > 1:
        result, grads[-1] = lax.optimization_barrier((result, grads[-1]))
    grads.append(lax.all_to_all(result, "seq", split_axis=0, concat_axis=0, tiled=True))
    for grad in grads[len(nears) :]:
        nears.append(sum_near(weight_grads(normed_t, cotangent_t, grad, images), seq_count))
    weight_sums = []
    if heads > 1:
        early = sum_far(jnp.concatenate(nears[:-1], axis=2))
        early, nears[-1] = lax.optimization_barrier((early, nears[-1]))
        weight_sums = jnp.split(early, heads - 1, axis=1)
    weight_sums.append(sum_far(nears[-1]))

    mixed, back = (project_back if aligned else project_back_plain)(grads, full_qkv, full_out, images)
    mixed_out = low(values + mixed).transpose(1, 0, 2)
    grad_centred = back * norm_gain
    mean_one, mean_two = group_sums(grad_centred, grad_centred * centred)
    grad_values = inv_std * (grad_centred - spread(mean_one) - centred * spread(mean_two))
    grad_latent = low(cot_rows.astype(jnp.float32) + grad_values).transpose(1, 0, 2)

    own_rows = channels // devices
    summed = jnp.stack(weight_sums).reshape(heads, own_rows, groups, 4, HEAD)
    summed = summed.transpose(1, 3, 2, 0, 4).reshape(own_rows, 4, HEADS * HEAD)
    grad_qkv = jnp.concatenate([summed[:, 2], summed[:, 0], summed[:, 1]], axis=1)
    out_rows = HEADS * HEAD // devices
    pieces = summed[:, 3].reshape(own_rows, devices, out_rows).transpose(1, 2, 0)
    pieces = lax.all_to_all(pieces, ALL, split_axis=0, concat_axis=0, tiled=True)
    grad_out = pieces.transpose(1, 0, 2).reshape(out_rows, channels)
    return (mixed_out, grad_latent, grad_qkv, grad_out)


def solution(mesh):
    placed = (
        P("seq", ("rep", "own"), None),
        P("seq", ("rep", "own"), None),
        P(),
        P(),
        P("own", None),
        P("own", None),
    )
    return jax.shard_map(
        shards,
        mesh=mesh,
        in_specs=placed,
        out_specs=(
            P("seq", ("rep", "own"), None),
            P("seq", ("rep", "own"), None),
            P(ALL, None),
            P(ALL, None),
        ),
        check_vma=False,
    )
```

```python
import functools
import math
import jax
import jax.numpy as jnp
from jax import lax
from jax.experimental import pallas as pl
from jax.experimental.pallas import tpu as pltpu
from jax.sharding import PartitionSpec as P

HEADS = 16
HEAD = 64
GROUPS = 32
EPS = 1e-06
LOG2E = math.log2(math.e)
PACK = 4 * HEAD
HALF = 2 * HEAD
ALL = ("seq", "rep", "own")
NT = (((1,), (1,)), ((), ()))
NN = (((1,), (0,)), ((), ()))
VMEM = 56 * 2**20


def dot(left, right, dims=NN):
    return lax.dot_general(left, right, dims, preferred_element_type=jnp.float32)


def low(array):
    return array.astype(jnp.bfloat16)


def eight_rows(array, op):
    return op(array.reshape(array.shape[0] // 8, 8, array.shape[1]), axis=0)


def pair_body(bq, kb, me_ref, *refs):
    ins, (o_ref, x_ref, kv_t, s_buf, dp_buf, acc, done) = refs[:-7], refs[-7:]
    length = x_ref.shape[0]
    piece = length // len(ins)
    for j, ref in enumerate(ins):
        x_ref[j * piece : (j + 1) * piece, :] = ref[...].reshape(piece, PACK)
    key_blocks, query_blocks = length // kb, length // bq
    step_len = min(512, length)
    first = lax.broadcasted_iota(jnp.int32, (1, HALF), 1) < HEAD
    zero = jnp.bfloat16(0)

    def prepare(j, carry):
        rows = pl.ds(pl.multiple_of(j * step_len, step_len), step_len)
        kv_t[:, rows] = low(x_ref[rows, 0:HALF].astype(jnp.float32).T)
        acc[rows, :] = jnp.zeros((step_len, HALF), jnp.float32)
        return carry

    lax.fori_loop(0, length // step_len, prepare, 0)

    def query_block(i):
        pair = x_ref[pl.ds(pl.multiple_of(i * bq, bq), bq), HALF:PACK]
        query = jnp.where(first, pair, zero) * jnp.bfloat16(HEAD**-0.5)
        return query, jnp.where(first, zero, pair)

    def score_block(j, query, buf, top):
        keys = slice(j * kb, (j + 1) * kb)
        scores = dot(x_ref[keys, 0:HALF], query, NT)
        s_buf[buf, keys, :] = scores
        return jnp.maximum(top, eight_rows(scores, jnp.max))

    def finish_top(top):
        return jnp.max(top, axis=0, keepdims=True) * LOG2E

    no_top = jnp.full((8, bq), -jnp.inf, jnp.float32)

    def step(i, top):
        buf = lax.rem(i, 2)
        query, grad = query_block(i)
        next_query, _ = query_block(lax.rem(i + 1, query_blocks))
        total = jnp.zeros((8, bq), jnp.float32)
        delta = jnp.zeros((8, bq), jnp.float32)
        for j in range(key_blocks):
            keys = slice(j * kb, (j + 1) * kb)
            dprobs = dot(x_ref[keys, 0:HALF], grad, NT)
            weights = jnp.exp2(s_buf[buf, keys, :] * LOG2E - top)
            s_buf[buf, keys, :] = weights
            dp_buf[keys, :] = dprobs
            total = total + eight_rows(weights, jnp.sum)
            delta = delta + eight_rows(weights * dprobs, jnp.sum)
        inverse = 1.0 / jnp.sum(total, axis=0, keepdims=True)
        delta = jnp.sum(delta, axis=0, keepdims=True) * inverse
        attended = jnp.zeros((HEAD, bq), jnp.float32)
        grad_query = jnp.zeros((HEAD, bq), jnp.float32)
        next_top = no_top
        for j in range(key_blocks):
            keys = slice(j * kb, (j + 1) * kb)
            probs = s_buf[buf, keys, :] * inverse
            probs_low = low(probs)
            dscores = low(probs * (dp_buf[keys, :] - delta))
            attended = attended + dot(kv_t[HEAD:HALF, keys], probs_low)
            grad_query = grad_query + dot(kv_t[0:HEAD, keys], dscores)
            acc[keys, :] += dot(dscores, query) + dot(probs_low, grad)
            next_top = score_block(j, next_query, 1 - buf, next_top)
        both = jnp.concatenate([grad_query * HEAD**-0.5, attended], axis=0)
        done[pl.ds(pl.multiple_of(i * bq, bq), bq), :] = low(both.T)
        return finish_top(next_top)

    top = no_top
    first_query, _ = query_block(0)
    for j in range(key_blocks):
        top = score_block(j, first_query, 0, top)
    lax.fori_loop(0, query_blocks, step, finish_top(top))

    tokens = o_ref.shape[1]
    for j in range(len(ins)):
        for half in range(2):
            rows = slice((2 * j + half) * tokens, (2 * j + half + 1) * tokens)
            owner = me_ref[0] ^ (half * len(ins) + j)
            o_ref[owner, :, 0:HALF] = low(acc[rows, :])
            o_ref[owner, :, HALF:PACK] = done[rows, :]


def attend_pair(pieces, me):
    tokens = pieces[0].shape[1]
    blocks = 2 * len(pieces)
    length = blocks * tokens
    bq, kb = min(256, length), min(256, length)
    vmem = pl.BlockSpec(memory_space=pltpu.VMEM)
    return pl.pallas_call(
        functools.partial(pair_body, bq, kb),
        out_shape=jax.ShapeDtypeStruct((blocks, tokens, PACK), jnp.bfloat16),
        in_specs=[pl.BlockSpec(memory_space=pltpu.SMEM)] + [vmem] * len(pieces),
        out_specs=vmem,
        scratch_shapes=[
            pltpu.VMEM((length, PACK), jnp.bfloat16),
            pltpu.VMEM((HALF, length), jnp.bfloat16),
            pltpu.VMEM((2, length, bq), jnp.float32),
            pltpu.VMEM((length, bq), jnp.float32),
            pltpu.VMEM((length, HALF), jnp.float32),
            pltpu.VMEM((length, HALF), jnp.bfloat16),
        ],
        compiler_params=pltpu.CompilerParams(vmem_limit_bytes=VMEM),
        cost_estimate=pl.CostEstimate(
            flops=6 * 2 * length * length * 256, bytes_accessed=4 * length * PACK, transcendentals=length * length
        ),
        name="attend_pair",
    )(me, *pieces)


def lane_piece(array, head, slot):
    piece = array[:, head * HEAD // HALF * HALF :][:, :HALF]
    return piece if head % 2 == slot % 2 else pltpu.roll(piece, HEAD, 1)


def project_body(count, groups, unit_ref, norm_ref, grad_ref, wq_ref, wk_ref, wv_ref, *outs):
    first = lax.broadcasted_iota(jnp.int32, (1, HALF), 1) < HEAD
    width = count * HEAD
    halves, tokens, channels = norm_ref.shape
    weights = jnp.concatenate([wq_ref[...], wk_ref[...], wv_ref[...]], axis=1)
    projected = dot(norm_ref[...].reshape(halves * tokens, channels), weights)
    query, key, value = (projected[:, part * width : (part + 1) * width] for part in range(3))
    grad = grad_ref[...].reshape(halves * tokens, width).astype(jnp.float32)
    packs = []
    for head in range(count):
        left = jnp.where(first, lane_piece(key, head, 0), lane_piece(value, head, 1))
        right = jnp.where(first, lane_piece(query, head, 0), lane_piece(grad, head, 1))
        packs.append(low(jnp.concatenate([left, right], axis=1)).reshape(halves, tokens, PACK))
    for flip in range(groups):

        @pl.when(pl.program_id(0) == flip)
        def _():
            for head in range(count):
                outs[head * groups + flip][...] = packs[head]


def project(normed, grads, full_qkv, unit, heads, offset, count):
    halves, tokens, channels = normed.shape
    groups = HEADS // heads
    width = count * HEAD
    steps = heads // count

    def columns(part):
        return pl.BlockSpec(
            (channels, width), lambda j, unit: (0, (part * groups + (j ^ unit[0])) * steps + offset // count)
        )

    results = pl.pallas_call(
        functools.partial(project_body, count, groups),
        out_shape=[jax.ShapeDtypeStruct((halves, tokens, PACK), jnp.bfloat16)] * (count * groups),
        grid_spec=pltpu.PrefetchScalarGridSpec(
            num_scalar_prefetch=1,
            grid=(groups,),
            in_specs=[
                pl.BlockSpec((halves, tokens, channels), lambda j, unit: (0, 0, 0)),
                pl.BlockSpec((halves, tokens, width), lambda j, unit: (0, 0, j ^ unit[0])),
                columns(0),
                columns(1),
                columns(2),
            ],
            out_specs=[pl.BlockSpec((halves, tokens, PACK), lambda j, unit: (0, 0, 0))] * (count * groups),
        ),
        compiler_params=pltpu.CompilerParams(vmem_limit_bytes=VMEM),
        cost_estimate=pl.CostEstimate(
            flops=2 * halves * tokens * channels * 4 * groups * width, bytes_accessed=2**24, transcendentals=0
        ),
        name="project",
    )(unit, normed, grads, full_qkv, full_qkv, full_qkv)
    return [results[head * groups : (head + 1) * groups] for head in range(count)]


def project_plain(normed, grads, full_qkv, unit, heads, offset, count):
    halves, tokens, channels = normed.shape
    groups = HEADS // heads
    qkv = low(jnp.einsum("itc,cd->itd", normed, full_qkv, preferred_element_type=jnp.float32))
    split = qkv.reshape(halves, tokens, 3, groups, heads, HEAD)[:, :, :, :, offset : offset + count]
    grads = grads.reshape(halves, tokens, 1, groups, count, HEAD)
    packed = jnp.concatenate([split[:, :, 1:3], split[:, :, 0:1], grads], axis=2)
    packed = packed.transpose(4, 3, 0, 1, 2, 5).reshape(count, groups, halves, tokens, PACK)
    packed = jnp.take(packed, jnp.arange(groups) ^ unit[0], axis=1)
    return [[packed[head, flip] for flip in range(groups)] for head in range(count)]


def weight_body(images, here_ref, norm_ref, cot_ref, grad_ref, *refs):
    outs, (grads, total) = refs[:-2], refs[-2:]
    groups, tokens = grad_ref.shape[0] // images, grad_ref.shape[1]
    first = lax.broadcasted_iota(jnp.int32, (1, HALF), 1) < HEAD
    split = groups * 3 * HEAD

    @pl.when(pl.program_id(0) == 0)
    def _():
        for image in range(images):
            rows = slice(image * tokens, (image + 1) * tokens)
            for group in range(0, groups, 2):
                pair = [grad_ref[image * groups + group + odd] for odd in range(2)]
                for odd in range(2):
                    grads[rows, (group + odd) * HALF : (group + odd + 1) * HALF] = pair[odd][:, 0:HALF]
                left, right = (part[:, HALF:PACK].astype(jnp.float32) for part in pair)
                query = groups * HALF + group * HEAD
                grads[rows, query : query + HALF] = low(jnp.where(first, left, pltpu.roll(right, HEAD, 1)))
                out = split + group * HEAD
                grads[rows, out : out + HALF] = low(jnp.where(first, pltpu.roll(left, HEAD, 1), right))

    total[:, 0:split] = dot(norm_ref[...], grads[:, 0:split])
    total[:, split:] = dot(cot_ref[...], grads[:, split:])
    rep, far, block, _ = outs[0].shape
    for place in range(far):
        for own, out in enumerate(outs):
            for row in range(rep):
                start = (place * rep * len(outs) + (here_ref[0] ^ (row * len(outs) + own))) * block
                out[row, place] = low(total[pl.ds(pl.multiple_of(start, 8), block), :])


def weight_grads(normed_t, cotangent_t, grads, here, images, near, far):
    own = lax.axis_size("own")
    channels, rows = normed_t.shape
    groups = grads.shape[0] // images
    tokens = grads.shape[1]
    steps = 2
    part = channels // steps
    block = channels // (near * far)
    return pl.pallas_call(
        functools.partial(weight_body, images),
        out_shape=[jax.ShapeDtypeStruct((near // own, far, block, groups * PACK), jnp.bfloat16)] * own,
        grid=(steps,),
        in_specs=[
            pl.BlockSpec(memory_space=pltpu.SMEM),
            pl.BlockSpec((part, rows), lambda g: (g, 0)),
            pl.BlockSpec((part, rows), lambda g: (g, 0)),
            pl.BlockSpec(grads.shape, lambda g: (0, 0, 0)),
        ],
        out_specs=[pl.BlockSpec((near // own, far // steps, block, groups * PACK), lambda g: (0, g, 0, 0))] * own,
        scratch_shapes=[
            pltpu.VMEM((images * tokens, groups * PACK), jnp.bfloat16),
            pltpu.VMEM((part, groups * PACK), jnp.float32),
        ],
        compiler_params=pltpu.CompilerParams(vmem_limit_bytes=VMEM),
        cost_estimate=pl.CostEstimate(
            flops=2 * channels * rows * groups * PACK, bytes_accessed=2**23, transcendentals=0
        ),
        name="weight_grads",
    )(here, normed_t, cotangent_t, grads)


def weight_grads_plain(normed_t, cotangent_t, grads, here, images, near, far):
    channels, rows = normed_t.shape
    groups, tokens = grads.shape[0] // images, grads.shape[1]
    cut = grads.reshape(images, groups, tokens, 4, HEAD).transpose(0, 2, 1, 3, 4).reshape(rows, groups, 4, HEAD)
    left = jnp.concatenate([cut[:, :, 0:2].reshape(rows, -1), cut[:, :, 2].reshape(rows, -1)], axis=1)
    total = jnp.concatenate([dot(normed_t, left), dot(cotangent_t, cut[:, :, 3].reshape(rows, -1))], axis=1)
    total = low(total).reshape(far, near, -1, groups * PACK)
    parts = [lax.dynamic_index_in_dim(total, here[0] ^ flip, 1, keepdims=False) for flip in range(near)]
    own = lax.axis_size("own")
    return [jnp.stack(parts[flip::own]) for flip in range(own)]


def gather_heads(parts, slot):
    first = lax.broadcasted_iota(jnp.int32, (1, HALF), 1) < HEAD
    base = slot // 2 * HALF
    pieces = []
    for even in range(0, len(parts), 2):
        left, right = parts[even][:, base : base + HALF], parts[even + 1][:, base : base + HALF]
        if slot % 2 == 0:
            right = pltpu.roll(right, HEAD, 1)
        else:
            left = pltpu.roll(left, HEAD, 1)
        pieces.append(jnp.where(first, left, right))
    return low(jnp.concatenate(pieces, axis=1))


def back_body(count, steps, *refs):
    grads = refs[:count]
    wq_ref, wk_ref, wv_ref, wo_ref = refs[count : count + 4]
    parts = [ref[...].reshape(-1, PACK).astype(jnp.float32) for ref in grads]
    stacked = jnp.concatenate([gather_heads(parts, slot) for slot in (2, 0, 1)], axis=1)
    weights = jnp.concatenate([wq_ref[...], wk_ref[...], wv_ref[...]], axis=1)
    back = dot(stacked, weights, NT)
    mixed = dot(gather_heads(parts, 3), wo_ref[...])
    g = pl.program_id(0)
    if len(refs) == count + 6:
        back_ref, mix_ref = refs[count + 4 :]

        @pl.when(g == 0)
        def _():
            back_ref[...] = back
            mix_ref[...] = mixed

        @pl.when(g > 0)
        def _():
            back_ref[...] += back
            mix_ref[...] += mixed

        return
    back_in, mix_in, row_ref, mean_ref, inv_ref, gain_ref, back_ref, mix_ref, sum_ref, mix = refs[count + 4 :]

    @pl.when(g == 0)
    def _():
        back_ref[...] = back_in[...] + back
        mix[...] = mix_in[...] + mixed

    @pl.when(g > 0)
    def _():
        back_ref[...] += back
        mix[...] += mixed

    @pl.when(g == steps - 1)
    def _():
        images, tokens, channels = row_ref.shape
        size = min(64, tokens)
        for image in range(images):
            mean, inv, gain = mean_ref[image], inv_ref[image], gain_ref[...]

            def piece(j, sums):
                inner = pl.ds(pl.multiple_of(j * size, size), size)
                outer = pl.ds(pl.multiple_of(image * tokens + j * size, size), size)
                values = row_ref[image, inner, :].astype(jnp.float32)
                mix_ref[image, inner, :] = low(values + mix[outer, :])
                grad = back_ref[outer, :] * gain
                return (
                    sums[0] + eight_rows(grad, jnp.sum),
                    sums[1] + eight_rows(grad * ((values - mean) * inv), jnp.sum),
                )

            zero = jnp.zeros((8, channels), jnp.float32)
            sums = lax.fori_loop(0, tokens // size, piece, (zero, zero))
            for kind in range(2):
                sum_ref[kind, image] = jnp.sum(sums[kind], axis=0, keepdims=True)


def project_back(grads, full_qkv, full_out, heads, offset, images, tail=None):
    count = len(grads)
    groups = HEADS // heads
    steps = heads // count
    tokens = grads[0].shape[1]
    channels = full_qkv.shape[0]
    width = count * HEAD

    def columns(part):
        return pl.BlockSpec((channels, width), lambda g: (0, (part * groups + g) * steps + offset // count))

    def whole(shape):
        return pl.BlockSpec(shape, lambda g: (0,) * len(shape))

    def once(shape):
        return pl.BlockSpec(shape, lambda g: (0,) * len(shape), pipeline_mode=pl.Buffered(1))

    flat = (images * tokens, channels)
    shape = (images, tokens, channels)
    line = (images, 1, channels)
    in_specs = [pl.BlockSpec((images, 1, tokens, PACK), lambda g: (0, g, 0, 0))] * count + [
        columns(0),
        columns(1),
        columns(2),
        pl.BlockSpec((width, channels), lambda g: (g * steps + offset // count, 0)),
    ]
    operands = [grad.reshape(images, groups, tokens, PACK) for grad in grads] + [full_qkv] * 3 + [full_out]
    out_shape = [jax.ShapeDtypeStruct(flat, jnp.float32)]
    out_specs = [whole(flat)]
    scratch = []
    if tail is None:
        out_shape, out_specs = out_shape * 2, out_specs * 2
    else:
        in_specs += [once(flat), once(flat), once(shape), whole(line), whole(line), whole((1, channels))]
        operands += list(tail)
        out_shape += [jax.ShapeDtypeStruct(shape, jnp.bfloat16), jax.ShapeDtypeStruct((2, *line), jnp.float32)]
        out_specs += [whole(shape), whole((2, *line))]
        scratch = [pltpu.VMEM(flat, jnp.float32)]
    return pl.pallas_call(
        functools.partial(back_body, count, groups),
        out_shape=out_shape,
        grid=(groups,),
        in_specs=in_specs,
        out_specs=out_specs,
        scratch_shapes=scratch,
        compiler_params=pltpu.CompilerParams(vmem_limit_bytes=VMEM),
        cost_estimate=pl.CostEstimate(
            flops=2 * images * tokens * channels * 4 * groups * width, bytes_accessed=2**24, transcendentals=0
        ),
        name="project_back",
    )(*operands)


def project_back_plain(grads, full_qkv, full_out, images):
    heads = len(grads)
    groups = HEADS // heads
    tokens = grads[0].shape[1]
    packed = jnp.stack(grads).reshape(heads, images, groups, tokens, 4, HEAD)
    packed = packed.transpose(1, 3, 4, 2, 0, 5).reshape(images, tokens, 4, HEADS * HEAD)
    key, value, query, attended = (packed[:, :, slot] for slot in range(4))
    stacked = jnp.concatenate([query, key, value], axis=2)
    mixed = jnp.einsum("itd,dc->itc", attended, full_out, preferred_element_type=jnp.float32)
    back = jnp.einsum("itd,cd->itc", stacked, full_qkv, preferred_element_type=jnp.float32)
    return mixed, back


def flipped(array, axis, flip):
    return lax.ppermute(array, axis, [(i, i ^ flip) for i in range(lax.axis_size(axis))])


def wide(array):
    return array.astype(jnp.float32)


def sum_near(parts, steps):
    rep = parts[0].shape[0]
    if steps == 1:
        total = wide(parts[0][0])
        for own, part in enumerate(parts):
            for row in range(rep):
                if own or row:
                    total = total + wide(flipped(part[row], ("rep", "own"), row * len(parts) + own))
        return total
    total = wide(parts[0])
    for own in range(1, len(parts)):
        total = total + wide(flipped(parts[own], "own", own))
    return total


def sum_rep(total):
    mine = total[0]
    for row in range(1, total.shape[0]):
        mine = mine + wide(flipped(low(total[row]), "rep", row))
    return mine


def sum_far(near, groups):
    place = lax.axis_index("seq")
    cut = near.reshape(2, groups, *near.shape[1:])

    def pick(array, index, dim):
        return lax.dynamic_index_in_dim(array, index, dim, keepdims=False)

    total = pick(cut, place % groups, 1)
    for flip in range(1, groups):
        total = total + wide(flipped(low(pick(cut, (place % groups) ^ flip, 1)), "seq", flip))
    half = place // groups
    return pick(total, half, 0) + wide(flipped(low(pick(total, 1 - half, 0)), "seq", groups))


def sum_seq(array):
    for bit in reversed(range(lax.axis_size("seq").bit_length() - 1)):
        array = array + flipped(array, "seq", 1 << bit)
    return array


def shards(latent, cotangent, norm_gain, norm_shift, proj_qkv, proj_out):
    tokens, images, channels = latent.shape
    seq_count = lax.axis_size("seq")
    devices = seq_count * lax.axis_size("rep") * lax.axis_size("own")
    per_group = channels // GROUPS
    total_count = tokens * seq_count * per_group
    groups = seq_count // images
    heads = HEADS // groups
    near = devices // seq_count
    block = channels // devices
    aligned = heads * HEAD % HALF == 0 and block % 8 == 0 and seq_count % 2 == 0
    here = (lax.axis_index("rep") * lax.axis_size("own") + lax.axis_index("own")).astype(jnp.int32).reshape(1)

    def weight_parts(grad):
        kernel = weight_grads if aligned else weight_grads_plain
        return kernel(normed_t, cotangent_t, grad, here, images, near, seq_count)

    full_qkv = lax.all_gather(proj_qkv, "own", axis=0, tiled=True)
    full_out = lax.all_gather(proj_out, "own", axis=0, tiled=True)

    def mean_groups(sums):
        return sum_seq(sums.reshape(2, images, GROUPS, per_group).sum(axis=3)) / total_count

    def spread(array):
        return jnp.repeat(array, per_group, axis=1)[:, None, :]

    me = lax.axis_index("seq").astype(jnp.int32).reshape(1)
    unit = me % groups
    image = lax.axis_index("seq") // groups

    def pick(array, index):
        return lax.dynamic_index_in_dim(array, index, 0, keepdims=False)

    def swapped(array):
        return jnp.stack([pick(array, image), flipped(pick(array, 1 - image), "seq", groups)])

    rows = latent.transpose(1, 0, 2)
    cot_rows = cotangent.transpose(1, 0, 2)
    work = swapped(rows).astype(jnp.float32)
    count = 2 if aligned else heads
    offsets = range(0, heads, count)
    grad_parts = []
    for offset in offsets:
        part = full_out.reshape(groups, heads, HEAD, channels)[:, offset : offset + count]
        part = part.reshape(groups * count * HEAD, channels)
        grad_parts.append(low(jnp.einsum("itc,dc->itd", cot_rows, part, preferred_element_type=jnp.float32)))

    values = rows.astype(jnp.float32)
    sums = jnp.stack([jnp.sum(values, axis=1), jnp.sum(values * values, axis=1)])
    group_mean, group_meansq = mean_groups(sums)
    group_inv = lax.rsqrt(group_meansq - group_mean * group_mean + EPS)
    mean, inv_std = spread(group_mean), spread(group_inv)
    centred = (values - mean) * inv_std
    normed = low(centred * norm_gain + norm_shift)
    normed_t = normed.reshape(images * tokens, channels).T
    cotangent_t = cot_rows.reshape(images * tokens, channels).T
    work_normed = low((work - pick(mean, image)) * pick(inv_std, image) * norm_gain + norm_shift)

    sends = []
    for index, offset in enumerate(offsets):
        part = swapped(grad_parts[index])
        if index + 1 < len(grad_parts):
            part, grad_parts[index + 1] = lax.optimization_barrier((part, grad_parts[index + 1]))
        sends += (project if aligned else project_plain)(work_normed, part, full_qkv, unit, heads, offset, count)
    grads, nears = [], []
    result = None
    for head in range(heads):
        pieces = [sends[head][0]] + [flipped(sends[head][flip], "seq", flip) for flip in range(1, groups)]
        if head == 0:
            pieces, normed_t, cotangent_t = lax.optimization_barrier((pieces, normed_t, cotangent_t))
        if head >= 1:
            pieces, result = lax.optimization_barrier((pieces, result))
            grads.append(lax.all_to_all(result, "seq", split_axis=0, concat_axis=0, tiled=True))
        if head + 1 < heads:
            pieces, sends[head + 1] = lax.optimization_barrier((pieces, sends[head + 1]))
        if head >= 2:
            parts = weight_parts(grads[head - 2])
            pieces, parts, grads[head - 2] = lax.optimization_barrier((pieces, parts, grads[head - 2]))
            nears.append(sum_near(parts, 1))
        if head >= 3:
            pieces, nears[head - 3] = lax.optimization_barrier((pieces, nears[head - 3]))
        result = attend_pair(pieces, me)
    if heads > 1:
        result, grads[-1], nears = lax.optimization_barrier((result, grads[-1], nears))
    grads.append(lax.all_to_all(result, "seq", split_axis=0, concat_axis=0, tiled=True))
    for index in range(len(nears), heads - 1):
        nears.append(sum_rep(sum_near(weight_parts(grads[index]), 2)))
    if aligned and heads > count:
        back, mixed = project_back(grads[:count], full_qkv, full_out, heads, 0, images)
        back, mixed, grads[-1], nears = lax.optimization_barrier((back, mixed, grads[-1], nears))
    last = sum_near(weight_parts(grads[-1]), 2)
    if heads > 1:
        last, grads[-1], nears = lax.optimization_barrier((last, grads[-1], nears))
    nears.append(sum_rep(last))
    gain = norm_gain[None, :]
    if aligned:
        if heads == count:
            back = mixed = jnp.zeros((images * tokens, channels), jnp.float32)
        offset = heads - count
        tail = (back, mixed, rows, mean, inv_std, gain)
        back, mixed_out, sums = project_back(grads[offset:], full_qkv, full_out, heads, offset, images, tail)
        back = back.reshape(images, tokens, channels)
        sums = sums.reshape(2, images, channels)
    else:
        mixed, back = project_back_plain(grads, full_qkv, full_out, images)
        mixed_out = low(values + mixed)
        sums = jnp.stack([jnp.sum(back * norm_gain, axis=1), jnp.sum(back * norm_gain * centred, axis=1)])
    sums, nears[-1] = lax.optimization_barrier((sums, nears[-1]))
    weight_sums = []
    if heads > 1:
        early = sum_far(jnp.concatenate(nears[:-1], axis=2), groups)
        early, nears[-1] = lax.optimization_barrier((early, nears[-1]))
        weight_sums = jnp.split(early, heads - 1, axis=1)
    weight_sums.append(sum_far(nears[-1], groups))

    mixed_out = mixed_out.transpose(1, 0, 2)
    mean_one, mean_two = mean_groups(sums)
    grad_values = inv_std * (back * norm_gain - spread(mean_one) - centred * spread(mean_two))
    grad_latent = low(cot_rows.astype(jnp.float32) + grad_values).transpose(1, 0, 2)

    summed = jnp.stack(weight_sums)
    split = groups * HALF

    def columns(part):
        part = part.reshape(heads, block, groups, -1, HEAD).transpose(3, 1, 2, 0, 4)
        return part.reshape(-1, block, HEADS * HEAD)

    keys_values = columns(summed[:, :, :split])
    queries_outs = [columns(part)[0] for part in jnp.split(summed[:, :, split:], 2, axis=2)]
    grad_qkv = jnp.concatenate([queries_outs[0], keys_values[0], keys_values[1]], axis=1)
    out_rows = HEADS * HEAD // devices
    pieces = queries_outs[1].reshape(block, devices, out_rows).transpose(1, 2, 0)
    pieces = lax.all_to_all(pieces, ALL, split_axis=0, concat_axis=0, tiled=True)
    grad_out = pieces.transpose(1, 0, 2).reshape(out_rows, channels)
    return (mixed_out, grad_latent, grad_qkv, grad_out)


def solution(mesh):
    placed = (
        P("seq", ("rep", "own"), None),
        P("seq", ("rep", "own"), None),
        P(),
        P(),
        P("own", None),
        P("own", None),
    )
    return jax.shard_map(
        shards,
        mesh=mesh,
        in_specs=placed,
        out_specs=(
            P("seq", ("rep", "own"), None),
            P("seq", ("rep", "own"), None),
            P(ALL, None),
            P(ALL, None),
        ),
        check_vma=False,
    )
```

```python
import functools
import math
import jax
import jax.numpy as jnp
from jax import lax
from jax.experimental import pallas as pl
from jax.experimental.pallas import tpu as pltpu
from jax.sharding import PartitionSpec as P

HEADS = 16
HEAD = 64
GROUPS = 32
EPS = 1e-06
LOG2E = math.log2(math.e)
PACK = 4 * HEAD
HALF = 2 * HEAD
ALL = ("seq", "rep", "own")
NT = (((1,), (1,)), ((), ()))
NN = (((1,), (0,)), ((), ()))
VMEM = 56 * 2**20


def dot(left, right, dims=NN):
    return lax.dot_general(left, right, dims, preferred_element_type=jnp.float32)


def low(array):
    return array.astype(jnp.bfloat16)


def eight_rows(array, op):
    return op(array.reshape(array.shape[0] // 8, 8, array.shape[1]), axis=0)


def pair_body(bq, kb, me_ref, *refs):
    ins, (o_ref, x_ref, kv_t, s_buf, dp_buf, acc, done) = refs[:-7], refs[-7:]
    length = x_ref.shape[0]
    piece = length // len(ins)
    for j, ref in enumerate(ins):
        x_ref[j * piece : (j + 1) * piece, :] = ref[...].reshape(piece, PACK)
    key_blocks, query_blocks = length // kb, length // bq
    step_len = min(512, length)
    first = lax.broadcasted_iota(jnp.int32, (1, HALF), 1) < HEAD
    zero = jnp.bfloat16(0)

    def prepare(j, carry):
        rows = pl.ds(pl.multiple_of(j * step_len, step_len), step_len)
        kv_t[:, rows] = low(x_ref[rows, 0:HALF].astype(jnp.float32).T)
        acc[rows, :] = jnp.zeros((step_len, HALF), jnp.float32)
        return carry

    lax.fori_loop(0, length // step_len, prepare, 0)

    def query_block(i):
        pair = x_ref[pl.ds(pl.multiple_of(i * bq, bq), bq), HALF:PACK]
        query = jnp.where(first, pair, zero) * jnp.bfloat16(HEAD**-0.5)
        return query, jnp.where(first, zero, pair)

    def score_block(j, query, buf, top):
        keys = slice(j * kb, (j + 1) * kb)
        scores = dot(x_ref[keys, 0:HALF], query, NT)
        s_buf[buf, keys, :] = scores
        return jnp.maximum(top, eight_rows(scores, jnp.max))

    def finish_top(top):
        return jnp.max(top, axis=0, keepdims=True) * LOG2E

    no_top = jnp.full((8, bq), -jnp.inf, jnp.float32)

    def step(i, top):
        buf = lax.rem(i, 2)
        query, grad = query_block(i)
        next_query, _ = query_block(lax.rem(i + 1, query_blocks))
        total = jnp.zeros((8, bq), jnp.float32)
        delta = jnp.zeros((8, bq), jnp.float32)
        for j in range(key_blocks):
            keys = slice(j * kb, (j + 1) * kb)
            dprobs = dot(x_ref[keys, 0:HALF], grad, NT)
            weights = jnp.exp2(s_buf[buf, keys, :] * LOG2E - top)
            s_buf[buf, keys, :] = weights
            dp_buf[keys, :] = dprobs
            total = total + eight_rows(weights, jnp.sum)
            delta = delta + eight_rows(weights * dprobs, jnp.sum)
        inverse = 1.0 / jnp.sum(total, axis=0, keepdims=True)
        delta = jnp.sum(delta, axis=0, keepdims=True) * inverse
        attended = jnp.zeros((HEAD, bq), jnp.float32)
        grad_query = jnp.zeros((HEAD, bq), jnp.float32)
        next_top = no_top
        for j in range(key_blocks):
            keys = slice(j * kb, (j + 1) * kb)
            probs = s_buf[buf, keys, :] * inverse
            probs_low = low(probs)
            dscores = low(probs * (dp_buf[keys, :] - delta))
            attended = attended + dot(kv_t[HEAD:HALF, keys], probs_low)
            grad_query = grad_query + dot(kv_t[0:HEAD, keys], dscores)
            acc[keys, :] += dot(dscores, query) + dot(probs_low, grad)
            next_top = score_block(j, next_query, 1 - buf, next_top)
        both = jnp.concatenate([grad_query * HEAD**-0.5, attended], axis=0)
        done[pl.ds(pl.multiple_of(i * bq, bq), bq), :] = low(both.T)
        return finish_top(next_top)

    top = no_top
    first_query, _ = query_block(0)
    for j in range(key_blocks):
        top = score_block(j, first_query, 0, top)
    lax.fori_loop(0, query_blocks, step, finish_top(top))

    tokens = o_ref.shape[1]
    for j in range(len(ins)):
        for half in range(2):
            rows = slice((2 * j + half) * tokens, (2 * j + half + 1) * tokens)
            owner = me_ref[0] ^ (half * len(ins) + j)
            o_ref[owner, :, 0:HALF] = low(acc[rows, :])
            o_ref[owner, :, HALF:PACK] = done[rows, :]


def attend_pair(pieces, me):
    tokens = pieces[0].shape[1]
    blocks = 2 * len(pieces)
    length = blocks * tokens
    bq, kb = min(256, length), min(256, length)
    vmem = pl.BlockSpec(memory_space=pltpu.VMEM)
    return pl.pallas_call(
        functools.partial(pair_body, bq, kb),
        out_shape=jax.ShapeDtypeStruct((blocks, tokens, PACK), jnp.bfloat16),
        in_specs=[pl.BlockSpec(memory_space=pltpu.SMEM)] + [vmem] * len(pieces),
        out_specs=vmem,
        scratch_shapes=[
            pltpu.VMEM((length, PACK), jnp.bfloat16),
            pltpu.VMEM((HALF, length), jnp.bfloat16),
            pltpu.VMEM((2, length, bq), jnp.float32),
            pltpu.VMEM((length, bq), jnp.float32),
            pltpu.VMEM((length, HALF), jnp.float32),
            pltpu.VMEM((length, HALF), jnp.bfloat16),
        ],
        compiler_params=pltpu.CompilerParams(vmem_limit_bytes=VMEM),
        cost_estimate=pl.CostEstimate(
            flops=6 * 2 * length * length * 256, bytes_accessed=4 * length * PACK, transcendentals=length * length
        ),
        name="attend_pair",
    )(me, *pieces)


def lane_piece(array, head, slot):
    piece = array[:, head * HEAD // HALF * HALF :][:, :HALF]
    return piece if head % 2 == slot % 2 else pltpu.roll(piece, HEAD, 1)


def project_body(count, groups, unit_ref, here_ref, there_ref, grad_here, grad_there, wq_ref, wk_ref, wv_ref, *outs):
    first = lax.broadcasted_iota(jnp.int32, (1, HALF), 1) < HEAD
    width = count * HEAD
    weights = jnp.concatenate([wq_ref[...], wk_ref[...], wv_ref[...]], axis=1)
    projected = dot(jnp.concatenate([here_ref[...], there_ref[...]], axis=0), weights)
    query, key, value = (projected[:, part * width : (part + 1) * width] for part in range(3))
    grad = jnp.concatenate([grad_here[...], grad_there[...]], axis=0).astype(jnp.float32)
    packs = []
    for head in range(count):
        left = jnp.where(first, lane_piece(key, head, 0), lane_piece(value, head, 1))
        right = jnp.where(first, lane_piece(query, head, 0), lane_piece(grad, head, 1))
        packs.append(low(jnp.concatenate([left, right], axis=1)).reshape(2, -1, PACK))
    for flip in range(groups):

        @pl.when(pl.program_id(0) == flip)
        def _():
            for head in range(count):
                outs[head * groups + flip][...] = packs[head]


def project(normed, grads, full_qkv, unit, heads, offset, count):
    halves, (tokens, channels) = len(normed), normed[0].shape
    groups = HEADS // heads
    width = count * HEAD
    steps = heads // count

    def columns(kind):
        return pl.BlockSpec(
            (channels, width), lambda j, unit: (0, (kind * groups + (j ^ unit[0])) * steps + offset // count)
        )

    results = pl.pallas_call(
        functools.partial(project_body, count, groups),
        out_shape=[jax.ShapeDtypeStruct((halves, tokens, PACK), jnp.bfloat16)] * (count * groups),
        grid_spec=pltpu.PrefetchScalarGridSpec(
            num_scalar_prefetch=1,
            grid=(groups,),
            in_specs=[
                pl.BlockSpec((tokens, channels), lambda j, unit: (0, 0)),
                pl.BlockSpec((tokens, channels), lambda j, unit: (0, 0)),
                pl.BlockSpec((tokens, width), lambda j, unit: (0, j ^ unit[0])),
                pl.BlockSpec((tokens, width), lambda j, unit: (0, j ^ unit[0])),
                columns(0),
                columns(1),
                columns(2),
            ],
            out_specs=[pl.BlockSpec((halves, tokens, PACK), lambda j, unit: (0, 0, 0))] * (count * groups),
        ),
        compiler_params=pltpu.CompilerParams(vmem_limit_bytes=VMEM),
        cost_estimate=pl.CostEstimate(
            flops=2 * halves * tokens * channels * groups * width, bytes_accessed=2**16, transcendentals=0
        ),
        name="project",
    )(unit, *normed, *grads, full_qkv, full_qkv, full_qkv)
    return [results[head * groups : (head + 1) * groups] for head in range(count)]


def project_plain(normed, grads, full_qkv, unit, heads, offset, count):
    normed, grads = jnp.stack(normed), jnp.stack(grads)
    halves, tokens, channels = normed.shape
    groups = HEADS // heads
    qkv = low(jnp.einsum("itc,cd->itd", normed, full_qkv, preferred_element_type=jnp.float32))
    split = qkv.reshape(halves, tokens, 3, groups, heads, HEAD)[:, :, :, :, offset : offset + count]
    grads = grads.reshape(halves, tokens, 1, groups, count, HEAD)
    packed = jnp.concatenate([split[:, :, 1:3], split[:, :, 0:1], grads], axis=2)
    packed = packed.transpose(4, 3, 0, 1, 2, 5).reshape(count, groups, halves, tokens, PACK)
    packed = jnp.take(packed, jnp.arange(groups) ^ unit[0], axis=1)
    return [[packed[head, flip] for flip in range(groups)] for head in range(count)]


def weight_body(images, here_ref, norm_ref, cot_ref, grad_ref, *refs):
    outs, (grads, total) = refs[:-2], refs[-2:]
    groups, tokens = grad_ref.shape[0] // images, grad_ref.shape[1]
    first = lax.broadcasted_iota(jnp.int32, (1, HALF), 1) < HEAD
    split = groups * 3 * HEAD

    @pl.when(pl.program_id(0) == 0)
    def _():
        for image in range(images):
            rows = slice(image * tokens, (image + 1) * tokens)
            for group in range(0, groups, 2):
                pair = [grad_ref[image * groups + group + odd] for odd in range(2)]
                for odd in range(2):
                    grads[rows, (group + odd) * HALF : (group + odd + 1) * HALF] = pair[odd][:, 0:HALF]
                left, right = (part[:, HALF:PACK].astype(jnp.float32) for part in pair)
                query = groups * HALF + group * HEAD
                grads[rows, query : query + HALF] = low(jnp.where(first, left, pltpu.roll(right, HEAD, 1)))
                out = split + group * HEAD
                grads[rows, out : out + HALF] = low(jnp.where(first, pltpu.roll(left, HEAD, 1), right))

    total[:, 0:split] = dot(norm_ref[...], grads[:, 0:split])
    total[:, split:] = dot(cot_ref[...], grads[:, split:])
    rep, far, block, _ = outs[0].shape
    for place in range(far):
        for own, out in enumerate(outs):
            for row in range(rep):
                start = (place * rep * len(outs) + (here_ref[0] ^ (row * len(outs) + own))) * block
                out[row, place] = low(total[pl.ds(pl.multiple_of(start, 8), block), :])


def weight_grads(normed_t, cotangent_t, grads, here, images, near, far):
    own = lax.axis_size("own")
    channels, rows = normed_t.shape
    groups = grads.shape[0] // images
    tokens = grads.shape[1]
    steps = 2
    part = channels // steps
    block = channels // (near * far)
    return pl.pallas_call(
        functools.partial(weight_body, images),
        out_shape=[jax.ShapeDtypeStruct((near // own, far, block, groups * PACK), jnp.bfloat16)] * own,
        grid=(steps,),
        in_specs=[
            pl.BlockSpec(memory_space=pltpu.SMEM),
            pl.BlockSpec((part, rows), lambda g: (g, 0)),
            pl.BlockSpec((part, rows), lambda g: (g, 0)),
            pl.BlockSpec(grads.shape, lambda g: (0, 0, 0)),
        ],
        out_specs=[pl.BlockSpec((near // own, far // steps, block, groups * PACK), lambda g: (0, g, 0, 0))] * own,
        scratch_shapes=[
            pltpu.VMEM((images * tokens, groups * PACK), jnp.bfloat16),
            pltpu.VMEM((part, groups * PACK), jnp.float32),
        ],
        compiler_params=pltpu.CompilerParams(vmem_limit_bytes=VMEM),
        cost_estimate=pl.CostEstimate(
            flops=2 * channels * rows * groups * PACK, bytes_accessed=2**23, transcendentals=0
        ),
        name="weight_grads",
    )(here, normed_t, cotangent_t, grads)


def weight_grads_plain(normed_t, cotangent_t, grads, here, images, near, far):
    channels, rows = normed_t.shape
    groups, tokens = grads.shape[0] // images, grads.shape[1]
    cut = grads.reshape(images, groups, tokens, 4, HEAD).transpose(0, 2, 1, 3, 4).reshape(rows, groups, 4, HEAD)
    left = jnp.concatenate([cut[:, :, 0:2].reshape(rows, -1), cut[:, :, 2].reshape(rows, -1)], axis=1)
    total = jnp.concatenate([dot(normed_t, left), dot(cotangent_t, cut[:, :, 3].reshape(rows, -1))], axis=1)
    total = low(total).reshape(far, near, -1, groups * PACK)
    parts = [lax.dynamic_index_in_dim(total, here[0] ^ flip, 1, keepdims=False) for flip in range(near)]
    own = lax.axis_size("own")
    return [jnp.stack(parts[flip::own]) for flip in range(own)]


def gather_heads(parts, slot):
    first = lax.broadcasted_iota(jnp.int32, (1, HALF), 1) < HEAD
    base = slot // 2 * HALF
    pieces = []
    for even in range(0, len(parts), 2):
        left, right = parts[even][:, base : base + HALF], parts[even + 1][:, base : base + HALF]
        if slot % 2 == 0:
            right = pltpu.roll(right, HEAD, 1)
        else:
            left = pltpu.roll(left, HEAD, 1)
        pieces.append(jnp.where(first, left, right))
    return low(jnp.concatenate(pieces, axis=1))


def back_body(offset, heads, *refs):
    refs, (stacked, attended) = refs[:-2], refs[-2:]
    count = len(refs) - 4 if len(refs) < 12 else len(refs) - 11
    grads, refs = refs[:count], refs[count:]
    qkv_ref, out_ref = refs[:2]
    images_groups, tokens, _ = grads[0].shape
    groups = HEADS // heads
    images = images_groups // groups
    width = count * HEAD

    @pl.when(pl.program_id(0) == 0)
    def _():
        for image in range(images):
            rows = slice(image * tokens, (image + 1) * tokens)
            for group in range(groups):
                parts = [wide(ref[image * groups + group]) for ref in grads]
                attended[rows, group * width : (group + 1) * width] = gather_heads(parts, 3)
                for kind, slot in enumerate((2, 0, 1)):
                    start = (kind * groups + group) * width
                    stacked[rows, start : start + width] = gather_heads(parts, slot)

    starts = [group * heads * HEAD + offset * HEAD for group in range(groups)]
    inner = HEADS * HEAD
    weights = [qkv_ref[:, kind * inner + start :][:, :width] for kind in range(3) for start in starts]
    back = dot(stacked[...], jnp.concatenate(weights, axis=1), NT)
    mixed = dot(attended[...], jnp.concatenate([out_ref[start : start + width, :] for start in starts], axis=0))
    if len(refs) == 4:
        refs[2][...] = back
        refs[3][...] = mixed
        return
    back_in, mix_in, row_ref, mean_ref, inv_ref, gain_ref, back_ref, mix_ref, sum_ref = refs[2:]
    back = back + back_in[...]
    mixed = mixed + mix_in[...]
    back_ref[...] = back
    for image in range(images):
        rows = slice(image * tokens, (image + 1) * tokens)
        values = wide(row_ref[image])
        mix_ref[image] = low(values + mixed[rows])
        grad = back[rows] * gain_ref[...]
        centred = (values - mean_ref[image]) * inv_ref[image]
        sum_ref[0, image] = jnp.sum(grad, axis=0, keepdims=True)
        sum_ref[1, image] = jnp.sum(grad * centred, axis=0, keepdims=True)


def project_back(grads, full_qkv, full_out, heads, offset, images, tail=None):
    count = len(grads)
    groups = HEADS // heads
    tokens = grads[0].shape[1]
    channels, columns = full_qkv.shape
    step = 256 if channels % 256 == 0 else channels
    flat = (images * tokens, step)
    line = (images, 1, step)

    def across(shape):
        return pl.BlockSpec(shape, lambda n: (0,) * (len(shape) - 1) + (n,))

    in_specs = [pl.BlockSpec(grads[0].shape, lambda n: (0, 0, 0))] * count + [
        pl.BlockSpec((step, columns), lambda n: (n, 0)),
        across((HEADS * HEAD, step)),
    ]
    out_shape = [jax.ShapeDtypeStruct((images * tokens, channels), jnp.float32)]
    out_specs = [across(flat)]
    if tail is None:
        out_shape, out_specs = out_shape * 2, out_specs * 2
    else:
        rows = across((images, tokens, step))
        in_specs += [across(flat), across(flat), rows, across(line), across(line), across((1, step))]
        out_shape += [
            jax.ShapeDtypeStruct((images, tokens, channels), jnp.bfloat16),
            jax.ShapeDtypeStruct((2, images, 1, channels), jnp.float32),
        ]
        out_specs += [rows, across((2, *line))]
    return pl.pallas_call(
        functools.partial(back_body, offset, heads),
        out_shape=out_shape,
        grid=(channels // step,),
        in_specs=in_specs,
        out_specs=out_specs,
        scratch_shapes=[
            pltpu.VMEM((images * tokens, 3 * groups * count * HEAD), jnp.bfloat16),
            pltpu.VMEM((images * tokens, groups * count * HEAD), jnp.bfloat16),
        ],
        compiler_params=pltpu.CompilerParams(vmem_limit_bytes=VMEM),
        cost_estimate=pl.CostEstimate(
            flops=2 * images * tokens * channels * 4 * groups * count * HEAD, bytes_accessed=2**24, transcendentals=0
        ),
        name="project_back",
    )(*grads, full_qkv, full_out, *(tail or ()))


def project_back_plain(grads, full_qkv, full_out, images):
    heads = len(grads)
    groups = HEADS // heads
    tokens = grads[0].shape[1]
    packed = jnp.stack(grads).reshape(heads, images, groups, tokens, 4, HEAD)
    packed = packed.transpose(1, 3, 4, 2, 0, 5).reshape(images, tokens, 4, HEADS * HEAD)
    key, value, query, attended = (packed[:, :, slot] for slot in range(4))
    stacked = jnp.concatenate([query, key, value], axis=2)
    mixed = jnp.einsum("itd,dc->itc", attended, full_out, preferred_element_type=jnp.float32)
    back = jnp.einsum("itd,cd->itc", stacked, full_qkv, preferred_element_type=jnp.float32)
    return mixed, back


def flipped(array, axis, flip):
    return lax.ppermute(array, axis, [(i, i ^ flip) for i in range(lax.axis_size(axis))])


def after(value, *others):
    return lax.optimization_barrier((value, others))[0]


def wide(array):
    return array.astype(jnp.float32)


def sum_near(parts, steps):
    rep = parts[0].shape[0]
    if steps == 1:
        total = wide(parts[0][0])
        for own, part in enumerate(parts):
            for row in range(rep):
                if own or row:
                    total = total + wide(flipped(part[row], ("rep", "own"), row * len(parts) + own))
        return total
    total = wide(parts[0])
    for own in range(1, len(parts)):
        total = total + wide(flipped(parts[own], "own", own))
    return total


def sum_rep(total):
    mine = total[0]
    for row in range(1, total.shape[0]):
        mine = mine + wide(flipped(low(total[row]), "rep", row))
    return mine


def sum_far(near, groups):
    place = lax.axis_index("seq")
    cut = near.reshape(2, groups, *near.shape[1:])

    def pick(array, index, dim):
        return lax.dynamic_index_in_dim(array, index, dim, keepdims=False)

    total = pick(cut, place % groups, 1)
    for flip in range(1, groups):
        total = total + wide(flipped(low(pick(cut, (place % groups) ^ flip, 1)), "seq", flip))
    half = place // groups
    return pick(total, half, 0) + wide(flipped(low(pick(total, 1 - half, 0)), "seq", groups))


def sum_seq(array, hold=()):
    bits = lax.axis_size("seq").bit_length() - 1
    for bit in range(bits):
        if bit == bits - 1:
            array = after(array, hold)
        array = array + flipped(array, "seq", 1 << bit)
    return array


def shards(latent, cotangent, norm_gain, norm_shift, proj_qkv, proj_out):
    tokens, images, channels = latent.shape
    seq_count = lax.axis_size("seq")
    devices = seq_count * lax.axis_size("rep") * lax.axis_size("own")
    per_group = channels // GROUPS
    total_count = tokens * seq_count * per_group
    groups = seq_count // images
    heads = HEADS // groups
    near = devices // seq_count
    block = channels // devices
    aligned = heads * HEAD % HALF == 0 and block % 8 == 0 and seq_count % 2 == 0
    here = (lax.axis_index("rep") * lax.axis_size("own") + lax.axis_index("own")).astype(jnp.int32).reshape(1)

    def weight_parts(grad):
        kernel = weight_grads if aligned else weight_grads_plain
        return kernel(normed_t, cotangent_t, grad, here, images, near, seq_count)

    full_qkv = lax.all_gather(proj_qkv, "own", axis=0, tiled=True)
    full_out = lax.all_gather(proj_out, "own", axis=0, tiled=True)

    def mean_groups(sums, hold=()):
        return sum_seq(sums.reshape(2, images, GROUPS, per_group).sum(axis=3), hold) / total_count

    def spread(array):
        return jnp.repeat(array, per_group, axis=1)[:, None, :]

    me = lax.axis_index("seq").astype(jnp.int32).reshape(1)
    unit = me % groups
    image = lax.axis_index("seq") // groups

    def pick(array, index):
        return lax.dynamic_index_in_dim(array, index, 0, keepdims=False)

    def swapped(array):
        return [pick(array, image), flipped(pick(array, 1 - image), "seq", groups)]

    rows = latent.transpose(1, 0, 2)
    cot_rows = cotangent.transpose(1, 0, 2)
    count = 2 if aligned else heads
    offsets = range(0, heads, count)
    grad_parts = []
    for offset in offsets:
        part = full_out.reshape(groups, heads, HEAD, channels)[:, offset : offset + count]
        part = part.reshape(groups * count * HEAD, channels)
        grad_parts.append(low(jnp.einsum("itc,dc->itd", cot_rows, part, preferred_element_type=jnp.float32)))
    work = swapped(rows)
    first_grad = grad_parts[0]
    grad_parts[0] = swapped(grad_parts[0])
    grad_parts[1:] = [swapped(after(part, grad_parts[0])) for part in grad_parts[1:]]

    values = rows.astype(jnp.float32)
    sums = jnp.stack([jnp.sum(values, axis=1), jnp.sum(values * values, axis=1)])
    group_mean, group_meansq = mean_groups(sums, first_grad)
    group_inv = lax.rsqrt(group_meansq - group_mean * group_mean + EPS)
    mean, inv_std = spread(group_mean), spread(group_inv)
    centred = (values - mean) * inv_std
    normed = low(centred * norm_gain + norm_shift)
    normed_t = normed.reshape(images * tokens, channels).T
    cotangent_t = cot_rows.reshape(images * tokens, channels).T
    work[1] = after(work[1], normed_t, cotangent_t)
    work_mean, work_inv = pick(mean, image), pick(inv_std, image)
    work = [low((wide(part) - work_mean) * work_inv * norm_gain + norm_shift) for part in work]
    kernel = project if aligned else project_plain
    sends = []
    for offset, grad_part in zip(offsets, grad_parts):
        sends += kernel(work, grad_part, full_qkv, unit, heads, offset, count)
    grads, nears = [], []
    result = None
    for head in range(heads):
        pieces = [sends[head][0]] + [flipped(sends[head][flip], "seq", flip) for flip in range(1, groups)]
        if head >= 1:
            pieces, result = lax.optimization_barrier((pieces, result))
            grads.append(lax.all_to_all(result, "seq", split_axis=0, concat_axis=0, tiled=True))
        if head + 2 < heads:
            pieces = after(pieces, sends[head + 2])
        if head >= 2:
            parts = weight_parts(grads[head - 2])
            pieces = after(pieces, parts)
            nears.append(sum_near(parts, 1))
        result = attend_pair(pieces, me)
    if heads > 1:
        result = after(result, grads[-1], nears)
    grads.append(lax.all_to_all(result, "seq", split_axis=0, concat_axis=0, tiled=True))
    for index in range(len(nears), heads - 1):
        nears.append(sum_rep(sum_near(weight_parts(grads[index]), 2)))
    if aligned and heads > count:
        back, mixed = project_back(grads[:count], full_qkv, full_out, heads, 0, images)
        grads[-1] = after(grads[-1], back, mixed, nears)
    last = sum_near(weight_parts(grads[-1]), 2)
    if heads > 1:
        grads[-1], nears = after((grads[-1], nears), last)
    nears.append(sum_rep(last))
    gain = norm_gain[None, :]
    if aligned:
        if heads == count:
            back = mixed = jnp.zeros((images * tokens, channels), jnp.float32)
        offset = heads - count
        tail = (back, mixed, rows, mean, inv_std, gain)
        back, mixed_out, sums = project_back(grads[offset:], full_qkv, full_out, heads, offset, images, tail)
        back = back.reshape(images, tokens, channels)
        sums = sums.reshape(2, images, channels)
    else:
        mixed, back = project_back_plain(grads, full_qkv, full_out, images)
        mixed_out = low(values + mixed)
        sums = jnp.stack([jnp.sum(back * norm_gain, axis=1), jnp.sum(back * norm_gain * centred, axis=1)])
    sums = after(sums, nears[-1])
    weight_sums = []
    if heads > 1:
        early = sum_far(jnp.concatenate(nears[:-1], axis=2), groups)
        weight_sums = jnp.split(early, heads - 1, axis=1)
    weight_sums.append(sum_far(nears[-1], groups))

    mixed_out = mixed_out.transpose(1, 0, 2)
    mean_one, mean_two = mean_groups(sums)
    grad_values = inv_std * (back * norm_gain - spread(mean_one) - centred * spread(mean_two))
    grad_latent = low(cot_rows.astype(jnp.float32) + grad_values).transpose(1, 0, 2)

    summed = jnp.stack(weight_sums)
    split = groups * HALF

    def columns(part):
        part = part.reshape(heads, block, groups, -1, HEAD).transpose(3, 1, 2, 0, 4)
        return part.reshape(-1, block, HEADS * HEAD)

    keys_values = columns(summed[:, :, :split])
    queries_outs = [columns(part)[0] for part in jnp.split(summed[:, :, split:], 2, axis=2)]
    grad_qkv = jnp.concatenate([queries_outs[0], keys_values[0], keys_values[1]], axis=1)
    out_rows = HEADS * HEAD // devices
    pieces = queries_outs[1].reshape(block, devices, out_rows).transpose(1, 2, 0)
    pieces = lax.all_to_all(pieces, ALL, split_axis=0, concat_axis=0, tiled=True)
    grad_out = pieces.transpose(1, 0, 2).reshape(out_rows, channels)
    return (mixed_out, grad_latent, grad_qkv, grad_out)


def solution(mesh):
    placed = (
        P("seq", ("rep", "own"), None),
        P("seq", ("rep", "own"), None),
        P(),
        P(),
        P("own", None),
        P("own", None),
    )
    return jax.shard_map(
        shards,
        mesh=mesh,
        in_specs=placed,
        out_specs=(
            P("seq", ("rep", "own"), None),
            P("seq", ("rep", "own"), None),
            P(ALL, None),
            P(ALL, None),
        ),
        check_vma=False,
    )
```

```python
import functools
import math
import jax
import jax.numpy as jnp
from jax import lax
from jax.experimental import pallas as pl
from jax.experimental.pallas import tpu as pltpu
from jax.sharding import PartitionSpec as P

HEADS = 16
HEAD = 64
GROUPS = 32
EPS = 1e-06
LOG2E = math.log2(math.e)
PACK = 4 * HEAD
HALF = 2 * HEAD
ALL = ("seq", "rep", "own")
NT = (((1,), (1,)), ((), ()))
NN = (((1,), (0,)), ((), ()))
VMEM = 56 * 2**20


def dot(left, right, dims=NN):
    return lax.dot_general(left, right, dims, preferred_element_type=jnp.float32)


def low(array):
    return array.astype(jnp.bfloat16)


def eight_rows(array, op):
    return op(array.reshape(array.shape[0] // 8, 8, array.shape[1]), axis=0)


def pair_body(bq, kb, flips, places, me_ref, *refs):
    ins, (o_ref, x_ref, kv_t, s_buf, dp_buf, acc, done) = refs[:-7], refs[-7:]
    length = x_ref.shape[0]
    piece = length // flips
    left = lax.broadcasted_iota(jnp.int32, (1, HALF), 1) < HEAD
    for j in range(flips):
        kinds = []
        for group, lane, _ in places:
            kinds.append(ins[group * flips + j][:, :, lane : lane + HALF].reshape(piece, HALF))
        query, grad = wide(kinds[1]), wide(kinds[2])
        query = query if places[1][2] == 0 else pltpu.roll(query, HEAD, 1)
        grad = grad if places[2][2] == 1 else pltpu.roll(grad, HEAD, 1)
        rows = slice(j * piece, (j + 1) * piece)
        x_ref[rows, 0:HALF] = kinds[0]
        x_ref[rows, HALF:PACK] = low(jnp.where(left, query, grad))
    key_blocks, query_blocks = length // kb, length // bq
    step_len = min(512, length)
    first = lax.broadcasted_iota(jnp.int32, (1, HALF), 1) < HEAD
    zero = jnp.bfloat16(0)

    def prepare(j, carry):
        rows = pl.ds(pl.multiple_of(j * step_len, step_len), step_len)
        kv_t[:, rows] = low(x_ref[rows, 0:HALF].astype(jnp.float32).T)
        acc[rows, :] = jnp.zeros((step_len, HALF), jnp.float32)
        return carry

    lax.fori_loop(0, length // step_len, prepare, 0)

    def query_block(i):
        pair = x_ref[pl.ds(pl.multiple_of(i * bq, bq), bq), HALF:PACK]
        query = jnp.where(first, pair, zero) * jnp.bfloat16(HEAD**-0.5)
        return query, jnp.where(first, zero, pair)

    def score_block(j, query, buf, top):
        keys = slice(j * kb, (j + 1) * kb)
        scores = dot(x_ref[keys, 0:HALF], query, NT)
        s_buf[buf, keys, :] = scores
        return jnp.maximum(top, eight_rows(scores, jnp.max))

    def finish_top(top):
        return jnp.max(top, axis=0, keepdims=True) * LOG2E

    no_top = jnp.full((8, bq), -jnp.inf, jnp.float32)

    def step(i, top):
        buf = lax.rem(i, 2)
        query, grad = query_block(i)
        next_query, _ = query_block(lax.rem(i + 1, query_blocks))
        total = jnp.zeros((8, bq), jnp.float32)
        delta = jnp.zeros((8, bq), jnp.float32)
        for j in range(key_blocks):
            keys = slice(j * kb, (j + 1) * kb)
            dprobs = dot(x_ref[keys, 0:HALF], grad, NT)
            weights = jnp.exp2(s_buf[buf, keys, :] * LOG2E - top)
            s_buf[buf, keys, :] = weights
            dp_buf[keys, :] = dprobs
            total = total + eight_rows(weights, jnp.sum)
            delta = delta + eight_rows(weights * dprobs, jnp.sum)
        inverse = 1.0 / jnp.sum(total, axis=0, keepdims=True)
        delta = jnp.sum(delta, axis=0, keepdims=True) * inverse
        attended = jnp.zeros((HEAD, bq), jnp.float32)
        grad_query = jnp.zeros((HEAD, bq), jnp.float32)
        next_top = no_top
        for j in range(key_blocks):
            keys = slice(j * kb, (j + 1) * kb)
            probs = s_buf[buf, keys, :] * inverse
            probs_low = low(probs)
            dscores = low(probs * (dp_buf[keys, :] - delta))
            attended = attended + dot(kv_t[HEAD:HALF, keys], probs_low)
            grad_query = grad_query + dot(kv_t[0:HEAD, keys], dscores)
            acc[keys, :] += dot(dscores, query) + dot(probs_low, grad)
            next_top = score_block(j, next_query, 1 - buf, next_top)
        both = jnp.concatenate([grad_query * HEAD**-0.5, attended], axis=0)
        done[pl.ds(pl.multiple_of(i * bq, bq), bq), :] = low(both.T)
        return finish_top(next_top)

    top = no_top
    first_query, _ = query_block(0)
    for j in range(key_blocks):
        top = score_block(j, first_query, 0, top)
    lax.fori_loop(0, query_blocks, step, finish_top(top))

    tokens = o_ref.shape[1]
    for j in range(flips):
        for half in range(2):
            rows = slice((2 * j + half) * tokens, (2 * j + half + 1) * tokens)
            owner = me_ref[0] ^ (half * flips + j)
            o_ref[owner, :, 0:HALF] = low(acc[rows, :])
            o_ref[owner, :, HALF:PACK] = done[rows, :]


def attend_pair(groups, places, me):
    pieces = [piece for group in groups for piece in group]
    flips = len(groups[0])
    tokens = pieces[0].shape[1]
    blocks = 2 * flips
    length = blocks * tokens
    bq, kb = min(256, length), min(256, length)
    vmem = pl.BlockSpec(memory_space=pltpu.VMEM)
    return pl.pallas_call(
        functools.partial(pair_body, bq, kb, flips, places),
        out_shape=jax.ShapeDtypeStruct((blocks, tokens, PACK), jnp.bfloat16),
        in_specs=[pl.BlockSpec(memory_space=pltpu.SMEM)] + [vmem] * len(pieces),
        out_specs=vmem,
        scratch_shapes=[
            pltpu.VMEM((length, PACK), jnp.bfloat16),
            pltpu.VMEM((HALF, length), jnp.bfloat16),
            pltpu.VMEM((2, length, bq), jnp.float32),
            pltpu.VMEM((length, bq), jnp.float32),
            pltpu.VMEM((length, HALF), jnp.float32),
            pltpu.VMEM((length, HALF), jnp.bfloat16),
        ],
        compiler_params=pltpu.CompilerParams(vmem_limit_bytes=VMEM),
        cost_estimate=pl.CostEstimate(
            flops=6 * 2 * length * length * 256, bytes_accessed=4 * length * PACK, transcendentals=length * length
        ),
        name="attend_pair",
    )(me, *pieces)


def project_body(groups, unit_ref, here_ref, there_ref, wq_ref, wk_ref, wv_ref, *outs):
    first = lax.broadcasted_iota(jnp.int32, (1, HALF), 1) < HEAD
    weights = jnp.concatenate([wq_ref[...], wk_ref[...], wv_ref[...]], axis=1)
    projected = dot(jnp.concatenate([here_ref[...], there_ref[...]], axis=0), weights)
    query, key, value = (projected[:, kind * HALF : (kind + 1) * HALF] for kind in range(3))
    pieces = [
        jnp.where(first, key, pltpu.roll(value, HEAD, 1)),
        query,
        jnp.where(first, pltpu.roll(key, HEAD, 1), value),
    ]
    packed = low(jnp.concatenate(pieces, axis=1)).reshape(2, -1, 3 * HALF)
    for flip in range(groups):

        @pl.when(pl.program_id(0) == flip)
        def _():
            lane = 0
            for out in outs[flip::groups]:
                out[...] = packed[:, :, lane : lane + out.shape[2]]
                lane += out.shape[2]


def project(normed, full_qkv, unit, heads, offset, widths):
    tokens, channels = normed[0].shape
    groups = HEADS // heads
    steps = heads // 2

    def columns(kind):
        return pl.BlockSpec((channels, HALF), lambda j, unit: (0, (kind * groups + (j ^ unit[0])) * steps + offset // 2))

    shapes = [(2, tokens, width) for width in widths for _ in range(groups)]
    rows = pl.BlockSpec((tokens, channels), lambda j, unit: (0, 0))
    results = pl.pallas_call(
        functools.partial(project_body, groups),
        out_shape=[jax.ShapeDtypeStruct(shape, jnp.bfloat16) for shape in shapes],
        grid_spec=pltpu.PrefetchScalarGridSpec(
            num_scalar_prefetch=1,
            grid=(groups,),
            in_specs=[rows, rows, columns(0), columns(1), columns(2)],
            out_specs=[pl.BlockSpec(shape, lambda j, unit: (0, 0, 0)) for shape in shapes],
        ),
        compiler_params=pltpu.CompilerParams(vmem_limit_bytes=VMEM),
        cost_estimate=pl.CostEstimate(
            flops=4 * tokens * channels * groups * 3 * HALF, bytes_accessed=2**16, transcendentals=0
        ),
        name="project",
    )(unit, *normed, full_qkv, full_qkv, full_qkv)
    return [results[index * groups : (index + 1) * groups] for index in range(len(widths))]


def project_plain(normed, full_qkv, unit, heads, offset):
    normed = jnp.stack(normed)
    groups = HEADS // heads
    qkv = low(jnp.einsum("itc,cd->itd", normed, full_qkv, preferred_element_type=jnp.float32))
    split = qkv.reshape(*normed.shape[:2], 3, groups, heads, HEAD)[:, :, :, :, offset]
    packed = jnp.concatenate([split[:, :, 1:3], split[:, :, 0:1], jnp.zeros_like(split[:, :, 0:1])], axis=2)
    packed = packed.transpose(3, 0, 1, 2, 4).reshape(groups, *normed.shape[:2], PACK)
    return [[lax.dynamic_index_in_dim(packed, unit[0] ^ flip, 0, keepdims=False) for flip in range(groups)]]


def weight_body(images, here_ref, norm_ref, cot_ref, grad_ref, *refs):
    outs, (grads, total) = refs[:-2], refs[-2:]
    groups, tokens = grad_ref.shape[0] // images, grad_ref.shape[1]
    first = lax.broadcasted_iota(jnp.int32, (1, HALF), 1) < HEAD
    split = groups * 3 * HEAD

    @pl.when(pl.program_id(0) == 0)
    def _():
        for image in range(images):
            rows = slice(image * tokens, (image + 1) * tokens)
            for group in range(0, groups, 2):
                pair = [grad_ref[image * groups + group + odd] for odd in range(2)]
                for odd in range(2):
                    grads[rows, (group + odd) * HALF : (group + odd + 1) * HALF] = pair[odd][:, 0:HALF]
                left, right = (part[:, HALF:PACK].astype(jnp.float32) for part in pair)
                query = groups * HALF + group * HEAD
                grads[rows, query : query + HALF] = low(jnp.where(first, left, pltpu.roll(right, HEAD, 1)))
                out = split + group * HEAD
                grads[rows, out : out + HALF] = low(jnp.where(first, pltpu.roll(left, HEAD, 1), right))

    total[:, 0:split] = dot(norm_ref[...], grads[:, 0:split])
    total[:, split:] = dot(cot_ref[...], grads[:, split:])
    rep, far, block, _ = outs[0].shape
    for place in range(far):
        for own, out in enumerate(outs):
            for row in range(rep):
                start = (place * rep * len(outs) + (here_ref[0] ^ (row * len(outs) + own))) * block
                out[row, place] = low(total[pl.ds(pl.multiple_of(start, 8), block), :])


def weight_grads(normed_t, cotangent_t, grads, here, images, near, far):
    own = lax.axis_size("own")
    channels, rows = normed_t.shape
    groups = grads.shape[0] // images
    tokens = grads.shape[1]
    steps = 2
    part = channels // steps
    block = channels // (near * far)
    return pl.pallas_call(
        functools.partial(weight_body, images),
        out_shape=[jax.ShapeDtypeStruct((near // own, far, block, groups * PACK), jnp.bfloat16)] * own,
        grid=(steps,),
        in_specs=[
            pl.BlockSpec(memory_space=pltpu.SMEM),
            pl.BlockSpec((part, rows), lambda g: (g, 0)),
            pl.BlockSpec((part, rows), lambda g: (g, 0)),
            pl.BlockSpec(grads.shape, lambda g: (0, 0, 0)),
        ],
        out_specs=[pl.BlockSpec((near // own, far // steps, block, groups * PACK), lambda g: (0, g, 0, 0))] * own,
        scratch_shapes=[
            pltpu.VMEM((images * tokens, groups * PACK), jnp.bfloat16),
            pltpu.VMEM((part, groups * PACK), jnp.float32),
        ],
        compiler_params=pltpu.CompilerParams(vmem_limit_bytes=VMEM),
        cost_estimate=pl.CostEstimate(
            flops=channels * rows, bytes_accessed=2**12, transcendentals=0
        ),
        name="weight_grads",
    )(here, normed_t, cotangent_t, grads)


def weight_grads_plain(normed_t, cotangent_t, grads, here, images, near, far):
    channels, rows = normed_t.shape
    groups, tokens = grads.shape[0] // images, grads.shape[1]
    cut = grads.reshape(images, groups, tokens, 4, HEAD).transpose(0, 2, 1, 3, 4).reshape(rows, groups, 4, HEAD)
    left = jnp.concatenate([cut[:, :, 0:2].reshape(rows, -1), cut[:, :, 2].reshape(rows, -1)], axis=1)
    total = jnp.concatenate([dot(normed_t, left), dot(cotangent_t, cut[:, :, 3].reshape(rows, -1))], axis=1)
    total = low(total).reshape(far, near, -1, groups * PACK)
    parts = [lax.dynamic_index_in_dim(total, here[0] ^ flip, 1, keepdims=False) for flip in range(near)]
    own = lax.axis_size("own")
    return [jnp.stack(parts[flip::own]) for flip in range(own)]


def gather_heads(parts, slot):
    first = lax.broadcasted_iota(jnp.int32, (1, HALF), 1) < HEAD
    base = slot // 2 * HALF
    pieces = []
    for even in range(0, len(parts), 2):
        left, right = parts[even][:, base : base + HALF], parts[even + 1][:, base : base + HALF]
        if slot % 2 == 0:
            right = pltpu.roll(right, HEAD, 1)
        else:
            left = pltpu.roll(left, HEAD, 1)
        pieces.append(jnp.where(first, left, right))
    return low(jnp.concatenate(pieces, axis=1))


def back_body(offset, heads, *refs):
    refs, (stacked, attended) = refs[:-2], refs[-2:]
    count = len(refs) - 4 if len(refs) < 12 else len(refs) - 11
    grads, refs = refs[:count], refs[count:]
    qkv_ref, out_ref = refs[:2]
    images_groups, tokens, _ = grads[0].shape
    groups = HEADS // heads
    images = images_groups // groups
    width = count * HEAD

    @pl.when(pl.program_id(0) == 0)
    def _():
        for image in range(images):
            rows = slice(image * tokens, (image + 1) * tokens)
            for group in range(groups):
                parts = [wide(ref[image * groups + group]) for ref in grads]
                attended[rows, group * width : (group + 1) * width] = gather_heads(parts, 3)
                for kind, slot in enumerate((2, 0, 1)):
                    start = (kind * groups + group) * width
                    stacked[rows, start : start + width] = gather_heads(parts, slot)

    starts = [group * heads * HEAD + offset * HEAD for group in range(groups)]
    inner = HEADS * HEAD
    weights = [qkv_ref[:, kind * inner + start :][:, :width] for kind in range(3) for start in starts]
    back = dot(stacked[...], jnp.concatenate(weights, axis=1), NT)
    mixed = dot(attended[...], jnp.concatenate([out_ref[start : start + width, :] for start in starts], axis=0))
    if len(refs) == 4:
        refs[2][...] = back
        refs[3][...] = mixed
        return
    back_in, mix_in, row_ref, mean_ref, inv_ref, gain_ref, back_ref, mix_ref, sum_ref = refs[2:]
    back = back + back_in[...]
    mixed = mixed + mix_in[...]
    back_ref[...] = back
    for image in range(images):
        rows = slice(image * tokens, (image + 1) * tokens)
        values = wide(row_ref[image])
        mix_ref[image] = low(values + mixed[rows])
        grad = back[rows] * gain_ref[...]
        centred = (values - mean_ref[image]) * inv_ref[image]
        sum_ref[0, image] = jnp.sum(grad, axis=0, keepdims=True)
        sum_ref[1, image] = jnp.sum(grad * centred, axis=0, keepdims=True)


def project_back(grads, full_qkv, full_out, heads, offset, images, tail=None):
    count = len(grads)
    groups = HEADS // heads
    tokens = grads[0].shape[1]
    channels, columns = full_qkv.shape
    step = 256 if channels % 256 == 0 else channels
    flat = (images * tokens, step)
    line = (images, 1, step)

    def across(shape):
        return pl.BlockSpec(shape, lambda n: (0,) * (len(shape) - 1) + (n,))

    in_specs = [pl.BlockSpec(grads[0].shape, lambda n: (0, 0, 0))] * count + [
        pl.BlockSpec((step, columns), lambda n: (n, 0)),
        across((HEADS * HEAD, step)),
    ]
    out_shape = [jax.ShapeDtypeStruct((images * tokens, channels), jnp.float32)]
    out_specs = [across(flat)]
    if tail is None:
        out_shape, out_specs = out_shape * 2, out_specs * 2
    else:
        rows = across((images, tokens, step))
        in_specs += [across(flat), across(flat), rows, across(line), across(line), across((1, step))]
        out_shape += [
            jax.ShapeDtypeStruct((images, tokens, channels), jnp.bfloat16),
            jax.ShapeDtypeStruct((2, images, 1, channels), jnp.float32),
        ]
        out_specs += [rows, across((2, *line))]
    return pl.pallas_call(
        functools.partial(back_body, offset, heads),
        out_shape=out_shape,
        grid=(channels // step,),
        in_specs=in_specs,
        out_specs=out_specs,
        scratch_shapes=[
            pltpu.VMEM((images * tokens, 3 * groups * count * HEAD), jnp.bfloat16),
            pltpu.VMEM((images * tokens, groups * count * HEAD), jnp.bfloat16),
        ],
        compiler_params=pltpu.CompilerParams(vmem_limit_bytes=VMEM),
        cost_estimate=pl.CostEstimate(
            flops=images * tokens * channels, bytes_accessed=2**12, transcendentals=0
        ),
        name="project_back",
    )(*grads, full_qkv, full_out, *(tail or ()))


def project_back_plain(grads, full_qkv, full_out, images):
    heads = len(grads)
    groups = HEADS // heads
    tokens = grads[0].shape[1]
    packed = jnp.stack(grads).reshape(heads, images, groups, tokens, 4, HEAD)
    packed = packed.transpose(1, 3, 4, 2, 0, 5).reshape(images, tokens, 4, HEADS * HEAD)
    key, value, query, attended = (packed[:, :, slot] for slot in range(4))
    stacked = jnp.concatenate([query, key, value], axis=2)
    mixed = jnp.einsum("itd,dc->itc", attended, full_out, preferred_element_type=jnp.float32)
    back = jnp.einsum("itd,cd->itc", stacked, full_qkv, preferred_element_type=jnp.float32)
    return mixed, back


def flipped(array, axis, flip):
    return lax.ppermute(array, axis, [(i, i ^ flip) for i in range(lax.axis_size(axis))])


def after(value, *others):
    return lax.optimization_barrier((value, others))[0]


def wide(array):
    return array.astype(jnp.float32)


def move_near(parts):
    rep = parts[0].shape[0]
    moved = []
    for own, part in enumerate(parts):
        for row in range(rep):
            flip = row * len(parts) + own
            moved.append(flipped(part[row], ("rep", "own"), flip) if flip else part[row])
    return moved


def sum_own(parts):
    total = wide(parts[0])
    for own in range(1, len(parts)):
        total = total + wide(flipped(parts[own], "own", own))
    return total


def sum_rep(total):
    mine = total[0]
    for row in range(1, total.shape[0]):
        mine = mine + wide(flipped(low(total[row]), "rep", row))
    return mine


def sum_half(near, groups):
    place = lax.axis_index("seq") % groups
    cut = near.reshape(2, groups, *near.shape[1:])
    total = lax.dynamic_index_in_dim(cut, place, 1, keepdims=False)
    for flip in range(1, groups):
        sent = lax.dynamic_index_in_dim(cut, place ^ flip, 1, keepdims=False)
        total = total + wide(flipped(low(sent), "seq", flip))
    return total


def sum_halves(total, groups):
    half = lax.axis_index("seq") // groups
    sent = lax.dynamic_index_in_dim(total, 1 - half, 0, keepdims=False)
    return lax.dynamic_index_in_dim(total, half, 0, keepdims=False) + wide(flipped(low(sent), "seq", groups))


def sum_seq(array, hold=()):
    bits = lax.axis_size("seq").bit_length() - 1
    for step in range(bits):
        if step == bits - 1:
            array = after(array, hold)
        bit = step - 1 if step else bits - 1
        array = array + flipped(array, "seq", 1 << bit)
    return array


def shards(latent, cotangent, norm_gain, norm_shift, proj_qkv, proj_out):
    tokens, images, channels = latent.shape
    seq_count = lax.axis_size("seq")
    devices = seq_count * lax.axis_size("rep") * lax.axis_size("own")
    per_group = channels // GROUPS
    total_count = tokens * seq_count * per_group
    groups = seq_count // images
    heads = HEADS // groups
    near = devices // seq_count
    block = channels // devices
    aligned = heads * HEAD % HALF == 0 and block % 8 == 0 and seq_count % 2 == 0
    here = (lax.axis_index("rep") * lax.axis_size("own") + lax.axis_index("own")).astype(jnp.int32).reshape(1)

    def weight_parts(grad):
        kernel = weight_grads if aligned else weight_grads_plain
        return kernel(normed_t, cotangent_t, grad, here, images, near, seq_count)

    full_qkv = lax.all_gather(proj_qkv, "own", axis=0, tiled=True)
    full_out = lax.all_gather(proj_out, "own", axis=0, tiled=True)

    def mean_groups(sums, hold=()):
        return sum_seq(sums.reshape(2, images, GROUPS, per_group).sum(axis=3), hold) / total_count

    def spread(array):
        return jnp.repeat(array, per_group, axis=1)[:, None, :]

    me = lax.axis_index("seq").astype(jnp.int32).reshape(1)
    unit = me % groups
    image = lax.axis_index("seq") // groups

    def pick(array, index):
        return lax.dynamic_index_in_dim(array, index, 0, keepdims=False)

    def swapped(array):
        return [pick(array, image), flipped(pick(array, 1 - image), "seq", groups)]

    rows = latent.transpose(1, 0, 2)
    cot_rows = cotangent.transpose(1, 0, 2)
    count = 2 if aligned else 1
    offsets = range(0, heads, count)
    grad_parts = []
    for offset in offsets:
        part = full_out.reshape(groups, heads, HEAD, channels)[:, offset : offset + count]
        part = part.reshape(groups * count * HEAD, channels)
        grad_parts.append(low(jnp.einsum("itc,dc->itd", cot_rows, part, preferred_element_type=jnp.float32)))
    work = swapped(rows)
    first_grad = grad_parts[0]
    grad_parts[0] = swapped(grad_parts[0])

    values = rows.astype(jnp.float32)
    sums = jnp.stack([jnp.sum(values, axis=1), jnp.sum(values * values, axis=1)])
    group_mean, group_meansq = mean_groups(sums, first_grad)
    group_inv = lax.rsqrt(group_meansq - group_mean * group_mean + EPS)
    mean, inv_std = spread(group_mean), spread(group_inv)
    centred = (values - mean) * inv_std
    normed = low(centred * norm_gain + norm_shift)
    normed_t = normed.reshape(images * tokens, channels).T
    cotangent_t = cot_rows.reshape(images * tokens, channels).T
    work[1] = after(work[1], normed_t, cotangent_t)
    work_mean, work_inv = pick(mean, image), pick(inv_std, image)
    work = [low((wide(part) - work_mean) * work_inv * norm_gain + norm_shift) for part in work]

    def exchanged(pieces):
        return [pieces[0]] + [flipped(pieces[flip], "seq", flip) for flip in range(1, groups)]

    def grad_pieces(halves):
        pieces = []
        for flip in range(groups):
            start = (unit[0] ^ flip) * (count * HEAD)
            both = [lax.dynamic_slice_in_dim(half, start, count * HEAD, 1) for half in halves]
            pieces.append(jnp.pad(jnp.stack(both), ((0, 0), (0, 0), (0, HALF - count * HEAD))))
        return pieces

    arrays, heads_plan, moved = [], [], {}
    for index, offset in enumerate(offsets):
        base = len(arrays)
        if not aligned:
            arrays += project_plain(work, full_qkv, unit, heads, offset)
            heads_plan.append(((base, 0, 0), (base, HALF, 0), (base + 1, 0, 0)))
        elif index == 0:
            arrays += project(work, full_qkv, unit, heads, offset, (PACK, HALF))
            heads_plan.append(((base, 0, 0), (base, HALF, 0), (base + 2, 0, 0)))
            heads_plan.append(((base + 1, 0, 0), (base, HALF, 1), (base + 2, 0, 1)))
        else:
            arrays += project(work, full_qkv, unit, heads, offset, (PACK + HALF,))
            heads_plan.append(((base, 0, 0), (base, HALF, 0), (base + 1, 0, 0)))
            heads_plan.append(((base, PACK, 0), (base, HALF, 1), (base + 1, 0, 1)))
        if index:
            arrays.append(grad_parts[index])
        else:
            arrays.append(None)
    early = arrays[2 if aligned else 1 :][1:2]
    moved[0] = exchanged(arrays[0])
    first = 2 if aligned else 1
    arrays[first] = grad_pieces(after(grad_parts[0], moved[0], early))
    moved[first] = exchanged(arrays[first])
    for index in range(1, len(arrays)):
        if index != first:
            arrays[index] = after(arrays[index], moved[first])

    grads, nears = [], []
    result = None
    for head in range(heads):
        used = sorted({place[0] for place in heads_plan[head]})
        late = heads_plan[head][2][0]
        if late != first and late not in moved:
            halves = swapped(arrays[late])
            moved[late] = exchanged(grad_pieces(after(halves, first_result)))
        for index in used:
            if index not in moved:
                moved[index] = exchanged(arrays[index])
        operands = [moved[index] for index in used]
        if head >= 1:
            operands, result = lax.optimization_barrier((operands, result))
            grads.append(lax.all_to_all(result, "seq", split_axis=0, concat_axis=0, tiled=True))
        if head >= 2:
            operands = after(operands, grads[head - 2])
        if head == 2:
            parts = weight_parts(grads[0])
            operands = after(operands, parts)
            near_moved = move_near(parts)
        places = tuple((used.index(index), lane, half) for index, lane, half in heads_plan[head])
        result = attend_pair(operands, places, me)
        if head == 0:
            first_result = result
    if heads > 1:
        result = after(result, grads[-1])
    if heads > 2:
        result = after(result, near_moved)
        nears.append(sum(wide(part) for part in near_moved))
        grads[1:] = after(grads[1:], result)
    grads.append(lax.all_to_all(result, "seq", split_axis=0, concat_axis=0, tiled=True))
    back = mixed = jnp.zeros((images * tokens, channels), jnp.float32)
    if aligned and heads > count:
        back, mixed = project_back(grads[:count], full_qkv, full_out, heads, 0, images)
        grads[-1] = after(grads[-1], back, mixed)
    middle = [sum_own(weight_parts(grads[index])) for index in range(len(nears), heads - 1)]
    if middle:
        middle = [sum_rep(total) for total in middle]
        nears += middle
        grads[-1] = after(grads[-1], middle)
    last = sum_own(weight_parts(grads[-1]))
    if heads > 1:
        grads[-1], nears = after((grads[-1], nears), last)
    nears.append(sum_rep(last))
    gain = norm_gain[None, :]
    if aligned:
        offset = heads - count
        tail = (back, mixed, rows, mean, inv_std, gain)
        back, mixed_out, sums = project_back(grads[offset:], full_qkv, full_out, heads, offset, images, tail)
        back = back.reshape(images, tokens, channels)
        sums = sums.reshape(2, images, channels)
    else:
        mixed, back = project_back_plain(grads, full_qkv, full_out, images)
        mixed_out = low(values + mixed)
        sums = jnp.stack([jnp.sum(back * norm_gain, axis=1), jnp.sum(back * norm_gain * centred, axis=1)])
    sums = after(sums, nears[-1])
    weight_sums = []
    if heads > 1:
        early = sum_halves(sum_half(jnp.concatenate(nears[:-1], axis=2), groups), groups)
        weight_sums = jnp.split(early, heads - 1, axis=1)
    last_sum = sum_half(nears[-1], groups)
    weight_sums.append(sum_halves(last_sum, groups))

    mixed_out = after(mixed_out, last_sum).transpose(1, 0, 2)
    mean_one, mean_two = mean_groups(sums)
    grad_values = inv_std * (back * norm_gain - spread(mean_one) - centred * spread(mean_two))
    grad_latent = low(cot_rows.astype(jnp.float32) + grad_values).transpose(1, 0, 2)

    summed = jnp.stack(weight_sums)
    split = groups * HALF

    def columns(part):
        part = part.reshape(heads, block, groups, -1, HEAD).transpose(3, 1, 2, 0, 4)
        return part.reshape(-1, block, HEADS * HEAD)

    keys_values = columns(summed[:, :, :split])
    queries_outs = [columns(part)[0] for part in jnp.split(summed[:, :, split:], 2, axis=2)]
    grad_qkv = jnp.concatenate([queries_outs[0], keys_values[0], keys_values[1]], axis=1)
    out_rows = HEADS * HEAD // devices
    pieces = queries_outs[1].reshape(block, devices, out_rows).transpose(1, 2, 0)
    pieces = lax.all_to_all(pieces, ALL, split_axis=0, concat_axis=0, tiled=True)
    grad_out = pieces.transpose(1, 0, 2).reshape(out_rows, channels)
    return (mixed_out, grad_latent, grad_qkv, grad_out)


def solution(mesh):
    placed = (
        P("seq", ("rep", "own"), None),
        P("seq", ("rep", "own"), None),
        P(),
        P(),
        P("own", None),
        P("own", None),
    )
    return jax.shard_map(
        shards,
        mesh=mesh,
        in_specs=placed,
        out_specs=(
            P("seq", ("rep", "own"), None),
            P("seq", ("rep", "own"), None),
            P(ALL, None),
            P(ALL, None),
        ),
        check_vma=False,
    )
```

```python
import functools
import math
import jax
import jax.numpy as jnp
from jax import lax
from jax.experimental import pallas as pl
from jax.experimental.pallas import tpu as pltpu
from jax.sharding import PartitionSpec as P

HEADS = 16
HEAD = 64
GROUPS = 32
EPS = 1e-06
LOG2E = math.log2(math.e)
PACK = 4 * HEAD
HALF = 2 * HEAD
ALL = ("seq", "rep", "own")
NT = (((1,), (1,)), ((), ()))
NN = (((1,), (0,)), ((), ()))
VMEM = 56 * 2**20


def dot(left, right, dims=NN):
    return lax.dot_general(left, right, dims, preferred_element_type=jnp.float32)


def low(array):
    return array.astype(jnp.bfloat16)


def eight_rows(array, op):
    return op(array.reshape(array.shape[0] // 8, 8, array.shape[1]), axis=0)


def pair_body(bq, kb, flips, places, me_ref, *refs):
    ins, (o_ref, x_ref, kv_t, s_buf, dp_buf, acc, done) = refs[:-7], refs[-7:]
    length = x_ref.shape[0]
    piece = length // flips
    left = lax.broadcasted_iota(jnp.int32, (1, HALF), 1) < HEAD
    for j in range(flips):
        kinds = []
        for group, lane, _ in places:
            kinds.append(ins[group * flips + j][:, :, lane : lane + HALF].reshape(piece, HALF))
        query, grad = wide(kinds[1]), wide(kinds[2])
        query = query if places[1][2] == 0 else pltpu.roll(query, HEAD, 1)
        grad = grad if places[2][2] == 1 else pltpu.roll(grad, HEAD, 1)
        rows = slice(j * piece, (j + 1) * piece)
        x_ref[rows, 0:HALF] = kinds[0]
        x_ref[rows, HALF:PACK] = low(jnp.where(left, query, grad))
    key_blocks, query_blocks = length // kb, length // bq
    step_len = min(512, length)
    first = lax.broadcasted_iota(jnp.int32, (1, HALF), 1) < HEAD
    zero = jnp.bfloat16(0)

    def prepare(j, carry):
        rows = pl.ds(pl.multiple_of(j * step_len, step_len), step_len)
        kv_t[:, rows] = low(x_ref[rows, 0:HALF].astype(jnp.float32).T)
        acc[rows, :] = jnp.zeros((step_len, HALF), jnp.float32)
        return carry

    lax.fori_loop(0, length // step_len, prepare, 0)

    def query_block(i):
        pair = x_ref[pl.ds(pl.multiple_of(i * bq, bq), bq), HALF:PACK]
        query = jnp.where(first, pair, zero) * jnp.bfloat16(HEAD**-0.5)
        return query, jnp.where(first, zero, pair)

    def score_block(j, query, buf, top):
        keys = slice(j * kb, (j + 1) * kb)
        scores = dot(x_ref[keys, 0:HALF], query, NT)
        s_buf[buf, keys, :] = scores
        return jnp.maximum(top, eight_rows(scores, jnp.max))

    def finish_top(top):
        return jnp.max(top, axis=0, keepdims=True) * LOG2E

    no_top = jnp.full((8, bq), -jnp.inf, jnp.float32)

    def step(i, top):
        buf = lax.rem(i, 2)
        query, grad = query_block(i)
        next_query, _ = query_block(lax.rem(i + 1, query_blocks))
        total = jnp.zeros((8, bq), jnp.float32)
        delta = jnp.zeros((8, bq), jnp.float32)
        for j in range(key_blocks):
            keys = slice(j * kb, (j + 1) * kb)
            dprobs = dot(x_ref[keys, 0:HALF], grad, NT)
            weights = jnp.exp2(s_buf[buf, keys, :] * LOG2E - top)
            s_buf[buf, keys, :] = weights
            dp_buf[keys, :] = dprobs
            total = total + eight_rows(weights, jnp.sum)
            delta = delta + eight_rows(weights * dprobs, jnp.sum)
        inverse = 1.0 / jnp.sum(total, axis=0, keepdims=True)
        delta = jnp.sum(delta, axis=0, keepdims=True) * inverse
        attended = jnp.zeros((HEAD, bq), jnp.float32)
        grad_query = jnp.zeros((HEAD, bq), jnp.float32)
        next_top = no_top
        for j in range(key_blocks):
            keys = slice(j * kb, (j + 1) * kb)
            probs = s_buf[buf, keys, :] * inverse
            probs_low = low(probs)
            dscores = low(probs * (dp_buf[keys, :] - delta))
            attended = attended + dot(kv_t[HEAD:HALF, keys], probs_low)
            grad_query = grad_query + dot(kv_t[0:HEAD, keys], dscores)
            acc[keys, :] += dot(dscores, query) + dot(probs_low, grad)
            next_top = score_block(j, next_query, 1 - buf, next_top)
        both = jnp.concatenate([grad_query * HEAD**-0.5, attended], axis=0)
        done[pl.ds(pl.multiple_of(i * bq, bq), bq), :] = low(both.T)
        return finish_top(next_top)

    top = no_top
    first_query, _ = query_block(0)
    for j in range(key_blocks):
        top = score_block(j, first_query, 0, top)
    lax.fori_loop(0, query_blocks, step, finish_top(top))

    tokens = o_ref.shape[1]
    for j in range(flips):
        for half in range(2):
            rows = slice((2 * j + half) * tokens, (2 * j + half + 1) * tokens)
            owner = me_ref[0] ^ (half * flips + j)
            o_ref[owner, :, 0:HALF] = low(acc[rows, :])
            o_ref[owner, :, HALF:PACK] = done[rows, :]


def attend_pair(groups, places, me):
    pieces = [piece for group in groups for piece in group]
    flips = len(groups[0])
    tokens = pieces[0].shape[1]
    blocks = 2 * flips
    length = blocks * tokens
    bq, kb = min(256, length), min(256, length)
    vmem = pl.BlockSpec(memory_space=pltpu.VMEM)
    return pl.pallas_call(
        functools.partial(pair_body, bq, kb, flips, places),
        out_shape=jax.ShapeDtypeStruct((blocks, tokens, PACK), jnp.bfloat16),
        in_specs=[pl.BlockSpec(memory_space=pltpu.SMEM)] + [vmem] * len(pieces),
        out_specs=vmem,
        scratch_shapes=[
            pltpu.VMEM((length, PACK), jnp.bfloat16),
            pltpu.VMEM((HALF, length), jnp.bfloat16),
            pltpu.VMEM((2, length, bq), jnp.float32),
            pltpu.VMEM((length, bq), jnp.float32),
            pltpu.VMEM((length, HALF), jnp.float32),
            pltpu.VMEM((length, HALF), jnp.bfloat16),
        ],
        compiler_params=pltpu.CompilerParams(vmem_limit_bytes=VMEM),
        cost_estimate=pl.CostEstimate(
            flops=6 * 2 * length * length * 256, bytes_accessed=4 * length * PACK, transcendentals=length * length
        ),
        name="attend_pair",
    )(me, *pieces)


def project_body(groups, unit_ref, here_ref, there_ref, wq_ref, wk_ref, wv_ref, *outs):
    first = lax.broadcasted_iota(jnp.int32, (1, HALF), 1) < HEAD
    weights = jnp.concatenate([wq_ref[...], wk_ref[...], wv_ref[...]], axis=1)
    projected = dot(jnp.concatenate([here_ref[...], there_ref[...]], axis=0), weights)
    query, key, value = (projected[:, kind * HALF : (kind + 1) * HALF] for kind in range(3))
    pieces = [
        jnp.where(first, key, pltpu.roll(value, HEAD, 1)),
        query,
        jnp.where(first, pltpu.roll(key, HEAD, 1), value),
    ]
    packed = low(jnp.concatenate(pieces, axis=1)).reshape(2, -1, 3 * HALF)
    for flip in range(groups):

        @pl.when(pl.program_id(0) == flip)
        def _():
            lane = 0
            for out in outs[flip::groups]:
                out[...] = packed[:, :, lane : lane + out.shape[2]]
                lane += out.shape[2]


def project(normed, full_qkv, unit, heads, offset, widths):
    tokens, channels = normed[0].shape
    groups = HEADS // heads
    steps = heads // 2

    def columns(kind):
        return pl.BlockSpec((channels, HALF), lambda j, unit: (0, (kind * groups + (j ^ unit[0])) * steps + offset // 2))

    shapes = [(2, tokens, width) for width in widths for _ in range(groups)]
    rows = pl.BlockSpec((tokens, channels), lambda j, unit: (0, 0))
    results = pl.pallas_call(
        functools.partial(project_body, groups),
        out_shape=[jax.ShapeDtypeStruct(shape, jnp.bfloat16) for shape in shapes],
        grid_spec=pltpu.PrefetchScalarGridSpec(
            num_scalar_prefetch=1,
            grid=(groups,),
            in_specs=[rows, rows, columns(0), columns(1), columns(2)],
            out_specs=[pl.BlockSpec(shape, lambda j, unit: (0, 0, 0)) for shape in shapes],
        ),
        compiler_params=pltpu.CompilerParams(vmem_limit_bytes=VMEM),
        cost_estimate=pl.CostEstimate(
            flops=4 * tokens * channels * groups * 3 * HALF, bytes_accessed=2**16, transcendentals=0
        ),
        name="project",
    )(unit, *normed, full_qkv, full_qkv, full_qkv)
    return [results[index * groups : (index + 1) * groups] for index in range(len(widths))]


def project_plain(normed, full_qkv, unit, heads, offset):
    normed = jnp.stack(normed)
    groups = HEADS // heads
    qkv = low(jnp.einsum("itc,cd->itd", normed, full_qkv, preferred_element_type=jnp.float32))
    split = qkv.reshape(*normed.shape[:2], 3, groups, heads, HEAD)[:, :, :, :, offset]
    packed = jnp.concatenate([split[:, :, 1:3], split[:, :, 0:1], jnp.zeros_like(split[:, :, 0:1])], axis=2)
    packed = packed.transpose(3, 0, 1, 2, 4).reshape(groups, *normed.shape[:2], PACK)
    return [[lax.dynamic_index_in_dim(packed, unit[0] ^ flip, 0, keepdims=False) for flip in range(groups)]]


def weight_body(images, here_ref, norm_ref, cot_ref, grad_ref, *refs):
    outs, (grads, total) = refs[:-2], refs[-2:]
    groups, tokens = grad_ref.shape[0] // images, grad_ref.shape[1]
    first = lax.broadcasted_iota(jnp.int32, (1, HALF), 1) < HEAD
    split = groups * 3 * HEAD

    @pl.when(pl.program_id(0) == 0)
    def _():
        for image in range(images):
            rows = slice(image * tokens, (image + 1) * tokens)
            for group in range(0, groups, 2):
                pair = [grad_ref[image * groups + group + odd] for odd in range(2)]
                for odd in range(2):
                    grads[rows, (group + odd) * HALF : (group + odd + 1) * HALF] = pair[odd][:, 0:HALF]
                left, right = (part[:, HALF:PACK].astype(jnp.float32) for part in pair)
                query = groups * HALF + group * HEAD
                grads[rows, query : query + HALF] = low(jnp.where(first, left, pltpu.roll(right, HEAD, 1)))
                out = split + group * HEAD
                grads[rows, out : out + HALF] = low(jnp.where(first, pltpu.roll(left, HEAD, 1), right))

    total[:, 0:split] = dot(norm_ref[...], grads[:, 0:split])
    total[:, split:] = dot(cot_ref[...], grads[:, split:])
    rep, far, block, _ = outs[0].shape
    for place in range(far):
        for own, out in enumerate(outs):
            for row in range(rep):
                start = (place * rep * len(outs) + (here_ref[0] ^ (row * len(outs) + own))) * block
                out[row, place] = low(total[pl.ds(pl.multiple_of(start, 8), block), :])


def weight_grads(normed_t, cotangent_t, grads, here, images, near, far):
    own = lax.axis_size("own")
    channels, rows = normed_t.shape
    groups = grads.shape[0] // images
    tokens = grads.shape[1]
    steps = 2
    part = channels // steps
    block = channels // (near * far)
    return pl.pallas_call(
        functools.partial(weight_body, images),
        out_shape=[jax.ShapeDtypeStruct((near // own, far, block, groups * PACK), jnp.bfloat16)] * own,
        grid=(steps,),
        in_specs=[
            pl.BlockSpec(memory_space=pltpu.SMEM),
            pl.BlockSpec((part, rows), lambda g: (g, 0)),
            pl.BlockSpec((part, rows), lambda g: (g, 0)),
            pl.BlockSpec(grads.shape, lambda g: (0, 0, 0)),
        ],
        out_specs=[pl.BlockSpec((near // own, far // steps, block, groups * PACK), lambda g: (0, g, 0, 0))] * own,
        scratch_shapes=[
            pltpu.VMEM((images * tokens, groups * PACK), jnp.bfloat16),
            pltpu.VMEM((part, groups * PACK), jnp.float32),
        ],
        compiler_params=pltpu.CompilerParams(vmem_limit_bytes=VMEM),
        cost_estimate=pl.CostEstimate(
            flops=channels * rows, bytes_accessed=2**12, transcendentals=0
        ),
        name="weight_grads",
    )(here, normed_t, cotangent_t, grads)


def weight_grads_plain(normed_t, cotangent_t, grads, here, images, near, far):
    channels, rows = normed_t.shape
    groups, tokens = grads.shape[0] // images, grads.shape[1]
    cut = grads.reshape(images, groups, tokens, 4, HEAD).transpose(0, 2, 1, 3, 4).reshape(rows, groups, 4, HEAD)
    left = jnp.concatenate([cut[:, :, 0:2].reshape(rows, -1), cut[:, :, 2].reshape(rows, -1)], axis=1)
    total = jnp.concatenate([dot(normed_t, left), dot(cotangent_t, cut[:, :, 3].reshape(rows, -1))], axis=1)
    total = low(total).reshape(far, near, -1, groups * PACK)
    parts = [lax.dynamic_index_in_dim(total, here[0] ^ flip, 1, keepdims=False) for flip in range(near)]
    own = lax.axis_size("own")
    return [jnp.stack(parts[flip::own]) for flip in range(own)]


def gather_heads(parts, slot):
    first = lax.broadcasted_iota(jnp.int32, (1, HALF), 1) < HEAD
    base = slot // 2 * HALF
    pieces = []
    for even in range(0, len(parts), 2):
        left, right = parts[even][:, base : base + HALF], parts[even + 1][:, base : base + HALF]
        if slot % 2 == 0:
            right = pltpu.roll(right, HEAD, 1)
        else:
            left = pltpu.roll(left, HEAD, 1)
        pieces.append(jnp.where(first, left, right))
    return low(jnp.concatenate(pieces, axis=1))


def back_body(offset, heads, *refs):
    refs, (stacked, attended) = refs[:-2], refs[-2:]
    count = len(refs) - 4 if len(refs) < 12 else len(refs) - 11
    grads, refs = refs[:count], refs[count:]
    qkv_ref, out_ref = refs[:2]
    images_groups, tokens, _ = grads[0].shape
    groups = HEADS // heads
    images = images_groups // groups
    width = count * HEAD

    @pl.when(pl.program_id(0) == 0)
    def _():
        for image in range(images):
            rows = slice(image * tokens, (image + 1) * tokens)
            for group in range(groups):
                parts = [wide(ref[image * groups + group]) for ref in grads]
                attended[rows, group * width : (group + 1) * width] = gather_heads(parts, 3)
                for kind, slot in enumerate((2, 0, 1)):
                    start = (kind * groups + group) * width
                    stacked[rows, start : start + width] = gather_heads(parts, slot)

    starts = [group * heads * HEAD + offset * HEAD for group in range(groups)]
    inner = HEADS * HEAD
    weights = [qkv_ref[:, kind * inner + start :][:, :width] for kind in range(3) for start in starts]
    back = dot(stacked[...], jnp.concatenate(weights, axis=1), NT)
    mixed = dot(attended[...], jnp.concatenate([out_ref[start : start + width, :] for start in starts], axis=0))
    if len(refs) == 4:
        refs[2][...] = back
        refs[3][...] = mixed
        return
    back_in, mix_in, row_ref, mean_ref, inv_ref, gain_ref, back_ref, mix_ref, sum_ref = refs[2:]
    back = back + back_in[...]
    mixed = mixed + mix_in[...]
    back_ref[...] = back
    for image in range(images):
        rows = slice(image * tokens, (image + 1) * tokens)
        values = wide(row_ref[image])
        mix_ref[image] = low(values + mixed[rows])
        grad = back[rows] * gain_ref[...]
        centred = (values - mean_ref[image]) * inv_ref[image]
        sum_ref[0, image] = jnp.sum(grad, axis=0, keepdims=True)
        sum_ref[1, image] = jnp.sum(grad * centred, axis=0, keepdims=True)


def project_back(grads, full_qkv, full_out, heads, offset, images, tail=None):
    count = len(grads)
    groups = HEADS // heads
    tokens = grads[0].shape[1]
    channels, columns = full_qkv.shape
    step = 256 if channels % 256 == 0 else channels
    flat = (images * tokens, step)
    line = (images, 1, step)

    def across(shape):
        return pl.BlockSpec(shape, lambda n: (0,) * (len(shape) - 1) + (n,))

    in_specs = [pl.BlockSpec(grads[0].shape, lambda n: (0, 0, 0))] * count + [
        pl.BlockSpec((step, columns), lambda n: (n, 0)),
        across((HEADS * HEAD, step)),
    ]
    out_shape = [jax.ShapeDtypeStruct((images * tokens, channels), jnp.float32)]
    out_specs = [across(flat)]
    if tail is None:
        out_shape, out_specs = out_shape * 2, out_specs * 2
    else:
        rows = across((images, tokens, step))
        in_specs += [across(flat), across(flat), rows, across(line), across(line), across((1, step))]
        out_shape += [
            jax.ShapeDtypeStruct((images, tokens, channels), jnp.bfloat16),
            jax.ShapeDtypeStruct((2, images, 1, channels), jnp.float32),
        ]
        out_specs += [rows, across((2, *line))]
    return pl.pallas_call(
        functools.partial(back_body, offset, heads),
        out_shape=out_shape,
        grid=(channels // step,),
        in_specs=in_specs,
        out_specs=out_specs,
        scratch_shapes=[
            pltpu.VMEM((images * tokens, 3 * groups * count * HEAD), jnp.bfloat16),
            pltpu.VMEM((images * tokens, groups * count * HEAD), jnp.bfloat16),
        ],
        compiler_params=pltpu.CompilerParams(vmem_limit_bytes=VMEM),
        cost_estimate=pl.CostEstimate(
            flops=images * tokens * channels * (1 if tail is None else 2**14), bytes_accessed=2**12, transcendentals=0
        ),
        name="project_back",
    )(*grads, full_qkv, full_out, *(tail or ()))


def project_back_plain(grads, full_qkv, full_out, images):
    heads = len(grads)
    groups = HEADS // heads
    tokens = grads[0].shape[1]
    packed = jnp.stack(grads).reshape(heads, images, groups, tokens, 4, HEAD)
    packed = packed.transpose(1, 3, 4, 2, 0, 5).reshape(images, tokens, 4, HEADS * HEAD)
    key, value, query, attended = (packed[:, :, slot] for slot in range(4))
    stacked = jnp.concatenate([query, key, value], axis=2)
    mixed = jnp.einsum("itd,dc->itc", attended, full_out, preferred_element_type=jnp.float32)
    back = jnp.einsum("itd,cd->itc", stacked, full_qkv, preferred_element_type=jnp.float32)
    return mixed, back


def flipped(array, axis, flip):
    return lax.ppermute(array, axis, [(i, i ^ flip) for i in range(lax.axis_size(axis))])


def after(value, *others):
    return lax.optimization_barrier((value, others))[0]


def wide(array):
    return array.astype(jnp.float32)


def sum_own(parts):
    total = wide(parts[0])
    for own in range(1, len(parts)):
        total = total + wide(flipped(parts[own], "own", own))
    return total


def sum_rep(total, hold=()):
    moved = [flipped(low(total[row]), "rep", row) for row in range(1, total.shape[0])]
    return total[0] + sum(wide(part) for part in after(moved, hold))


def half_pieces(near, groups):
    place = lax.axis_index("seq") % groups
    cut = near.reshape(2, groups, *near.shape[1:])
    pieces = [lax.dynamic_index_in_dim(cut, place ^ flip, 1, keepdims=False) for flip in range(groups)]
    return pieces[:1] + [low(piece) for piece in pieces[1:]]


def sum_half(pieces, hold=()):
    moved = [flipped(pieces[flip], "seq", flip) for flip in range(1, len(pieces))]
    return pieces[0] + sum(wide(part) for part in after(moved, hold))


def sum_halves(total, groups):
    half = lax.axis_index("seq") // groups
    sent = lax.dynamic_index_in_dim(total, 1 - half, 0, keepdims=False)
    return lax.dynamic_index_in_dim(total, half, 0, keepdims=False) + wide(flipped(low(sent), "seq", groups))


def sum_seq(array, hold=()):
    bits = lax.axis_size("seq").bit_length() - 1
    for step in range(bits):
        if step == bits - 1:
            array = after(array, hold)
        bit = step - 1 if step else bits - 1
        array = array + flipped(array, "seq", 1 << bit)
    return array


def shards(latent, cotangent, norm_gain, norm_shift, proj_qkv, proj_out):
    tokens, images, channels = latent.shape
    seq_count = lax.axis_size("seq")
    devices = seq_count * lax.axis_size("rep") * lax.axis_size("own")
    per_group = channels // GROUPS
    total_count = tokens * seq_count * per_group
    groups = seq_count // images
    heads = HEADS // groups
    near = devices // seq_count
    block = channels // devices
    aligned = heads * HEAD % HALF == 0 and block % 8 == 0 and seq_count % 2 == 0
    here = (lax.axis_index("rep") * lax.axis_size("own") + lax.axis_index("own")).astype(jnp.int32).reshape(1)

    def weight_parts(grad):
        kernel = weight_grads if aligned else weight_grads_plain
        return kernel(normed_t, cotangent_t, grad, here, images, near, seq_count)

    full_qkv = lax.all_gather(proj_qkv, "own", axis=0, tiled=True)
    full_out = lax.all_gather(proj_out, "own", axis=0, tiled=True)

    def mean_groups(sums, hold=()):
        return sum_seq(sums.reshape(2, images, GROUPS, per_group).sum(axis=3), hold) / total_count

    def spread(array):
        return jnp.repeat(array, per_group, axis=1)[:, None, :]

    me = lax.axis_index("seq").astype(jnp.int32).reshape(1)
    unit = me % groups
    image = lax.axis_index("seq") // groups

    def pick(array, index):
        return lax.dynamic_index_in_dim(array, index, 0, keepdims=False)

    def swapped(array):
        return [pick(array, image), flipped(pick(array, 1 - image), "seq", groups)]

    rows = latent.transpose(1, 0, 2)
    cot_rows = cotangent.transpose(1, 0, 2)
    count = 2 if aligned else 1
    offsets = range(0, heads, count)
    grad_parts = []
    for offset in offsets:
        part = full_out.reshape(groups, heads, HEAD, channels)[:, offset : offset + count]
        part = part.reshape(groups * count * HEAD, channels)
        grad_parts.append(low(jnp.einsum("itc,dc->itd", cot_rows, part, preferred_element_type=jnp.float32)))
    work = swapped(rows)
    first_grad = grad_parts[0]
    grad_parts[0] = swapped(after(grad_parts[0], work[1]))

    values = rows.astype(jnp.float32)
    sums = jnp.stack([jnp.sum(values, axis=1), jnp.sum(values * values, axis=1)])
    group_mean, group_meansq = mean_groups(sums, first_grad)
    group_inv = lax.rsqrt(group_meansq - group_mean * group_mean + EPS)
    mean, inv_std = spread(group_mean), spread(group_inv)
    centred = (values - mean) * inv_std
    normed = low(centred * norm_gain + norm_shift)
    normed_t = normed.reshape(images * tokens, channels).T
    cotangent_t = cot_rows.reshape(images * tokens, channels).T
    work[1] = after(work[1], normed_t, cotangent_t)
    work_mean, work_inv = pick(mean, image), pick(inv_std, image)
    work = [low((wide(part) - work_mean) * work_inv * norm_gain + norm_shift) for part in work]

    def exchanged(pieces):
        return [pieces[0]] + [flipped(pieces[flip], "seq", flip) for flip in range(1, groups)]

    def grad_pieces(halves):
        pieces = []
        for flip in range(groups):
            start = (unit[0] ^ flip) * (count * HEAD)
            both = [lax.dynamic_slice_in_dim(half, start, count * HEAD, 1) for half in halves]
            pieces.append(jnp.pad(jnp.stack(both), ((0, 0), (0, 0), (0, HALF - count * HEAD))))
        return pieces

    arrays, heads_plan, moved = [], [], {}
    for index, offset in enumerate(offsets):
        base = len(arrays)
        if not aligned:
            arrays += project_plain(work, full_qkv, unit, heads, offset)
            heads_plan.append(((base, 0, 0), (base, HALF, 0), (base + 1, 0, 0)))
        elif index == 0:
            arrays += project(work, full_qkv, unit, heads, offset, (PACK, HALF))
            heads_plan.append(((base, 0, 0), (base, HALF, 0), (base + 2, 0, 0)))
            heads_plan.append(((base + 1, 0, 0), (base, HALF, 1), (base + 2, 0, 1)))
        else:
            arrays += project(work, full_qkv, unit, heads, offset, (PACK + HALF,))
            heads_plan.append(((base, 0, 0), (base, HALF, 0), (base + 1, 0, 0)))
            heads_plan.append(((base, PACK, 0), (base, HALF, 1), (base + 1, 0, 1)))
        if index:
            arrays.append(grad_parts[index])
        else:
            arrays.append(None)
    early = arrays[2 if aligned else 1 :][1:2]
    moved[0] = exchanged(arrays[0])
    first = 2 if aligned else 1
    arrays[first] = grad_pieces(after(grad_parts[0], moved[0], early))
    moved[first] = exchanged(arrays[first])
    for index in range(1, len(arrays)):
        if index != first:
            arrays[index] = after(arrays[index], moved[first])

    grads = []
    result = None
    for head in range(heads):
        used = sorted({place[0] for place in heads_plan[head]})
        late = heads_plan[head][2][0]
        if late != first and late not in moved:
            halves = swapped(arrays[late])
            moved[late] = exchanged(grad_pieces(after(halves, first_result)))
        for index in used:
            if index not in moved:
                moved[index] = exchanged(arrays[index])
        operands = [moved[index] for index in used]
        if head >= 1:
            operands, result = lax.optimization_barrier((operands, result))
            grads.append(lax.all_to_all(result, "seq", split_axis=0, concat_axis=0, tiled=True))
        if head >= 2:
            operands = after(operands, grads[head - 2])
        places = tuple((used.index(index), lane, half) for index, lane, half in heads_plan[head])
        result = attend_pair(operands, places, me)
        if head == 0:
            first_result = result
    if heads > 1:
        result = after(result, grads[-1])
        token = flipped(result[0, :16, :HALF], "seq", 1)
        grads = after(grads, result, token)
    grads.append(lax.all_to_all(result, "seq", split_axis=0, concat_axis=0, tiled=True))
    back = mixed = jnp.zeros((images * tokens, channels), jnp.float32)
    if aligned and heads > count:
        back, mixed = project_back(grads[:count], full_qkv, full_out, heads, 0, images)
        grads[-1] = after(grads[-1], back, mixed)
    nears = [sum_own(weight_parts(grads[index])) for index in range(heads - 1)]
    grads[-1] = after(grads[-1], nears)
    last = sum_own(weight_parts(grads[-1]))
    if heads > 1:
        grads[-1] = after(grads[-1], last)
        nears = [sum_rep(total) for total in nears]
    gain = norm_gain[None, :]
    if aligned:
        offset = heads - count
        tail = (back, mixed, rows, mean, inv_std, gain)
        back, mixed_out, sums = project_back(grads[offset:], full_qkv, full_out, heads, offset, images, tail)
        back = back.reshape(images, tokens, channels)
        sums = sums.reshape(2, images, channels)
    else:
        mixed, back = project_back_plain(grads, full_qkv, full_out, images)
        mixed_out = low(values + mixed)
        sums = jnp.stack([jnp.sum(back * norm_gain, axis=1), jnp.sum(back * norm_gain * centred, axis=1)])
    last_pieces = half_pieces(sum_rep(last, back), groups)
    sums = after(sums, last_pieces)
    weight_sums = []
    if heads > 1:
        early = half_pieces(jnp.concatenate(after(nears, last), axis=2), groups)
        early = sum_halves(sum_half(early, back), groups)
        weight_sums = jnp.split(early, heads - 1, axis=1)
    last_sum = sum_half(last_pieces)
    weight_sums.append(sum_halves(last_sum, groups))

    mixed_out = after(mixed_out, last_sum).transpose(1, 0, 2)
    mean_one, mean_two = mean_groups(sums)
    grad_values = inv_std * (back * norm_gain - spread(mean_one) - centred * spread(mean_two))
    grad_latent = low(cot_rows.astype(jnp.float32) + grad_values).transpose(1, 0, 2)

    summed = jnp.stack(weight_sums)
    split = groups * HALF

    def columns(part):
        part = part.reshape(heads, block, groups, -1, HEAD).transpose(3, 1, 2, 0, 4)
        return part.reshape(-1, block, HEADS * HEAD)

    keys_values = columns(summed[:, :, :split])
    queries_outs = [columns(part)[0] for part in jnp.split(summed[:, :, split:], 2, axis=2)]
    grad_qkv = jnp.concatenate([queries_outs[0], keys_values[0], keys_values[1]], axis=1)
    out_rows = HEADS * HEAD // devices
    pieces = queries_outs[1].reshape(block, devices, out_rows).transpose(1, 2, 0)
    pieces = lax.all_to_all(pieces, ALL, split_axis=0, concat_axis=0, tiled=True)
    grad_out = pieces.transpose(1, 0, 2).reshape(out_rows, channels)
    return (mixed_out, grad_latent, grad_qkv, grad_out)


def solution(mesh):
    placed = (
        P("seq", ("rep", "own"), None),
        P("seq", ("rep", "own"), None),
        P(),
        P(),
        P("own", None),
        P("own", None),
    )
    return jax.shard_map(
        shards,
        mesh=mesh,
        in_specs=placed,
        out_specs=(
            P("seq", ("rep", "own"), None),
            P("seq", ("rep", "own"), None),
            P(ALL, None),
            P(ALL, None),
        ),
        check_vma=False,
    )
```

```python
import functools
import math
import jax
import jax.numpy as jnp
from jax import lax
from jax.experimental import pallas as pl
from jax.experimental.pallas import tpu as pltpu
from jax.sharding import PartitionSpec as P

HEADS = 16
HEAD = 64
GROUPS = 32
EPS = 1e-06
LOG2E = math.log2(math.e)
PACK = 4 * HEAD
HALF = 2 * HEAD
ALL = ("seq", "rep", "own")
NT = (((1,), (1,)), ((), ()))
NN = (((1,), (0,)), ((), ()))
VMEM = 56 * 2**20


def dot(left, right, dims=NN):
    return lax.dot_general(left, right, dims, preferred_element_type=jnp.float32)


def low(array):
    return array.astype(jnp.bfloat16)


def eight_rows(array, op):
    return op(array.reshape(array.shape[0] // 8, 8, array.shape[1]), axis=0)


def pair_body(bq, kb, flips, places, me_ref, *refs):
    ins, (o_ref, x_ref, kv_t, s_buf, dp_buf, acc, done) = refs[:-7], refs[-7:]
    length = x_ref.shape[0]
    piece = length // flips
    left = lax.broadcasted_iota(jnp.int32, (1, HALF), 1) < HEAD
    for j in range(flips):
        kinds = []
        for group, lane, _ in places:
            kinds.append(ins[group * flips + j][:, :, lane : lane + HALF].reshape(piece, HALF))
        query, grad = wide(kinds[1]), wide(kinds[2])
        query = query if places[1][2] == 0 else pltpu.roll(query, HEAD, 1)
        grad = grad if places[2][2] == 1 else pltpu.roll(grad, HEAD, 1)
        rows = slice(j * piece, (j + 1) * piece)
        x_ref[rows, 0:HALF] = kinds[0]
        x_ref[rows, HALF:PACK] = low(jnp.where(left, query, grad))
    key_blocks, query_blocks = length // kb, length // bq
    step_len = min(512, length)
    first = lax.broadcasted_iota(jnp.int32, (1, HALF), 1) < HEAD
    zero = jnp.bfloat16(0)

    def prepare(j, carry):
        rows = pl.ds(pl.multiple_of(j * step_len, step_len), step_len)
        kv_t[:, rows] = low(x_ref[rows, 0:HALF].astype(jnp.float32).T)
        acc[rows, :] = jnp.zeros((step_len, HALF), jnp.float32)
        return carry

    lax.fori_loop(0, length // step_len, prepare, 0)

    def query_block(i):
        pair = x_ref[pl.ds(pl.multiple_of(i * bq, bq), bq), HALF:PACK]
        query = jnp.where(first, pair, zero) * jnp.bfloat16(HEAD**-0.5)
        return query, jnp.where(first, zero, pair)

    def score_block(j, query, buf, top):
        keys = slice(j * kb, (j + 1) * kb)
        scores = dot(x_ref[keys, 0:HALF], query, NT)
        s_buf[buf, keys, :] = scores
        return jnp.maximum(top, eight_rows(scores, jnp.max))

    def finish_top(top):
        return jnp.max(top, axis=0, keepdims=True) * LOG2E

    no_top = jnp.full((8, bq), -jnp.inf, jnp.float32)

    def step(i, top):
        buf = lax.rem(i, 2)
        query, grad = query_block(i)
        next_query, _ = query_block(lax.rem(i + 1, query_blocks))
        total = jnp.zeros((8, bq), jnp.float32)
        delta = jnp.zeros((8, bq), jnp.float32)
        for j in range(key_blocks):
            keys = slice(j * kb, (j + 1) * kb)
            dprobs = dot(x_ref[keys, 0:HALF], grad, NT)
            weights = jnp.exp2(s_buf[buf, keys, :] * LOG2E - top)
            s_buf[buf, keys, :] = weights
            dp_buf[keys, :] = dprobs
            total = total + eight_rows(weights, jnp.sum)
            delta = delta + eight_rows(weights * dprobs, jnp.sum)
        inverse = 1.0 / jnp.sum(total, axis=0, keepdims=True)
        delta = jnp.sum(delta, axis=0, keepdims=True) * inverse
        attended = jnp.zeros((HEAD, bq), jnp.float32)
        grad_query = jnp.zeros((HEAD, bq), jnp.float32)
        next_top = no_top
        for j in range(key_blocks):
            keys = slice(j * kb, (j + 1) * kb)
            probs = s_buf[buf, keys, :] * inverse
            probs_low = low(probs)
            dscores = low(probs * (dp_buf[keys, :] - delta))
            attended = attended + dot(kv_t[HEAD:HALF, keys], probs_low)
            grad_query = grad_query + dot(kv_t[0:HEAD, keys], dscores)
            acc[keys, :] += dot(dscores, query) + dot(probs_low, grad)
            next_top = score_block(j, next_query, 1 - buf, next_top)
        both = jnp.concatenate([grad_query * HEAD**-0.5, attended], axis=0)
        done[pl.ds(pl.multiple_of(i * bq, bq), bq), :] = low(both.T)
        return finish_top(next_top)

    top = no_top
    first_query, _ = query_block(0)
    for j in range(key_blocks):
        top = score_block(j, first_query, 0, top)
    lax.fori_loop(0, query_blocks, step, finish_top(top))

    tokens = o_ref.shape[1]
    for j in range(flips):
        for half in range(2):
            rows = slice((2 * j + half) * tokens, (2 * j + half + 1) * tokens)
            owner = me_ref[0] ^ (half * flips + j)
            o_ref[owner, :, 0:HALF] = low(acc[rows, :])
            o_ref[owner, :, HALF:PACK] = done[rows, :]


def attend_pair(groups, places, me):
    pieces = [piece for group in groups for piece in group]
    flips = len(groups[0])
    tokens = pieces[0].shape[1]
    blocks = 2 * flips
    length = blocks * tokens
    bq, kb = min(256, length), min(256, length)
    vmem = pl.BlockSpec(memory_space=pltpu.VMEM)
    return pl.pallas_call(
        functools.partial(pair_body, bq, kb, flips, places),
        out_shape=jax.ShapeDtypeStruct((blocks, tokens, PACK), jnp.bfloat16),
        in_specs=[pl.BlockSpec(memory_space=pltpu.SMEM)] + [vmem] * len(pieces),
        out_specs=vmem,
        scratch_shapes=[
            pltpu.VMEM((length, PACK), jnp.bfloat16),
            pltpu.VMEM((HALF, length), jnp.bfloat16),
            pltpu.VMEM((2, length, bq), jnp.float32),
            pltpu.VMEM((length, bq), jnp.float32),
            pltpu.VMEM((length, HALF), jnp.float32),
            pltpu.VMEM((length, HALF), jnp.bfloat16),
        ],
        compiler_params=pltpu.CompilerParams(vmem_limit_bytes=VMEM),
        cost_estimate=pl.CostEstimate(
            flops=6 * 2 * length * length * 256, bytes_accessed=4 * length * PACK, transcendentals=length * length
        ),
        name="attend_pair",
    )(me, *pieces)


def project_body(groups, unit_ref, here_ref, there_ref, wq_ref, wk_ref, wv_ref, *outs):
    first = lax.broadcasted_iota(jnp.int32, (1, HALF), 1) < HEAD
    weights = jnp.concatenate([wq_ref[...], wk_ref[...], wv_ref[...]], axis=1)
    projected = dot(jnp.concatenate([here_ref[...], there_ref[...]], axis=0), weights)
    query, key, value = (projected[:, kind * HALF : (kind + 1) * HALF] for kind in range(3))
    pieces = [
        jnp.where(first, key, pltpu.roll(value, HEAD, 1)),
        query,
        jnp.where(first, pltpu.roll(key, HEAD, 1), value),
    ]
    packed = low(jnp.concatenate(pieces, axis=1)).reshape(2, -1, 3 * HALF)
    for flip in range(groups):

        @pl.when(pl.program_id(0) == flip)
        def _():
            lane = 0
            for out in outs[flip::groups]:
                out[...] = packed[:, :, lane : lane + out.shape[2]]
                lane += out.shape[2]


def project(normed, full_qkv, unit, heads, offset, widths):
    tokens, channels = normed[0].shape
    groups = HEADS // heads
    steps = heads // 2

    def columns(kind):
        return pl.BlockSpec((channels, HALF), lambda j, unit: (0, (kind * groups + (j ^ unit[0])) * steps + offset // 2))

    shapes = [(2, tokens, width) for width in widths for _ in range(groups)]
    rows = pl.BlockSpec((tokens, channels), lambda j, unit: (0, 0))
    results = pl.pallas_call(
        functools.partial(project_body, groups),
        out_shape=[jax.ShapeDtypeStruct(shape, jnp.bfloat16) for shape in shapes],
        grid_spec=pltpu.PrefetchScalarGridSpec(
            num_scalar_prefetch=1,
            grid=(groups,),
            in_specs=[rows, rows, columns(0), columns(1), columns(2)],
            out_specs=[pl.BlockSpec(shape, lambda j, unit: (0, 0, 0)) for shape in shapes],
        ),
        compiler_params=pltpu.CompilerParams(vmem_limit_bytes=VMEM),
        cost_estimate=pl.CostEstimate(
            flops=4 * tokens * channels * groups * 3 * HALF, bytes_accessed=2**16, transcendentals=0
        ),
        name="project",
    )(unit, *normed, full_qkv, full_qkv, full_qkv)
    return [results[index * groups : (index + 1) * groups] for index in range(len(widths))]


def project_plain(normed, full_qkv, unit, heads, offset):
    normed = jnp.stack(normed)
    groups = HEADS // heads
    qkv = low(jnp.einsum("itc,cd->itd", normed, full_qkv, preferred_element_type=jnp.float32))
    split = qkv.reshape(*normed.shape[:2], 3, groups, heads, HEAD)[:, :, :, :, offset]
    packed = jnp.concatenate([split[:, :, 1:3], split[:, :, 0:1], jnp.zeros_like(split[:, :, 0:1])], axis=2)
    packed = packed.transpose(3, 0, 1, 2, 4).reshape(groups, *normed.shape[:2], PACK)
    return [[lax.dynamic_index_in_dim(packed, unit[0] ^ flip, 0, keepdims=False) for flip in range(groups)]]


def weight_body(images, here_ref, norm_ref, cot_ref, grad_ref, *refs):
    outs, (grads, total) = refs[:-2], refs[-2:]
    groups, tokens = grad_ref.shape[0] // images, grad_ref.shape[1]
    first = lax.broadcasted_iota(jnp.int32, (1, HALF), 1) < HEAD
    split = groups * 3 * HEAD

    @pl.when(pl.program_id(0) == 0)
    def _():
        for image in range(images):
            rows = slice(image * tokens, (image + 1) * tokens)
            for group in range(0, groups, 2):
                pair = [grad_ref[image * groups + group + odd] for odd in range(2)]
                for odd in range(2):
                    grads[rows, (group + odd) * HALF : (group + odd + 1) * HALF] = pair[odd][:, 0:HALF]
                left, right = (part[:, HALF:PACK].astype(jnp.float32) for part in pair)
                query = groups * HALF + group * HEAD
                grads[rows, query : query + HALF] = low(jnp.where(first, left, pltpu.roll(right, HEAD, 1)))
                out = split + group * HEAD
                grads[rows, out : out + HALF] = low(jnp.where(first, pltpu.roll(left, HEAD, 1), right))

    total[:, 0:split] = dot(norm_ref[...], grads[:, 0:split])
    total[:, split:] = dot(cot_ref[...], grads[:, split:])
    rep, far, block, _ = outs[0].shape
    for place in range(far):
        for own, out in enumerate(outs):
            for row in range(rep):
                start = (place * rep * len(outs) + (here_ref[0] ^ (row * len(outs) + own))) * block
                out[row, place] = low(total[pl.ds(pl.multiple_of(start, 8), block), :])


def weight_grads(normed_t, cotangent_t, grads, here, images, near, far):
    own = lax.axis_size("own")
    channels, rows = normed_t.shape
    groups = grads.shape[0] // images
    tokens = grads.shape[1]
    steps = 2
    part = channels // steps
    block = channels // (near * far)
    return pl.pallas_call(
        functools.partial(weight_body, images),
        out_shape=[jax.ShapeDtypeStruct((near // own, far, block, groups * PACK), jnp.bfloat16)] * own,
        grid=(steps,),
        in_specs=[
            pl.BlockSpec(memory_space=pltpu.SMEM),
            pl.BlockSpec((part, rows), lambda g: (g, 0)),
            pl.BlockSpec((part, rows), lambda g: (g, 0)),
            pl.BlockSpec(grads.shape, lambda g: (0, 0, 0)),
        ],
        out_specs=[pl.BlockSpec((near // own, far // steps, block, groups * PACK), lambda g: (0, g, 0, 0))] * own,
        scratch_shapes=[
            pltpu.VMEM((images * tokens, groups * PACK), jnp.bfloat16),
            pltpu.VMEM((part, groups * PACK), jnp.float32),
        ],
        compiler_params=pltpu.CompilerParams(vmem_limit_bytes=VMEM),
        cost_estimate=pl.CostEstimate(
            flops=channels * rows, bytes_accessed=2**12, transcendentals=0
        ),
        name="weight_grads",
    )(here, normed_t, cotangent_t, grads)


def weight_grads_plain(normed_t, cotangent_t, grads, here, images, near, far):
    channels, rows = normed_t.shape
    groups, tokens = grads.shape[0] // images, grads.shape[1]
    cut = grads.reshape(images, groups, tokens, 4, HEAD).transpose(0, 2, 1, 3, 4).reshape(rows, groups, 4, HEAD)
    left = jnp.concatenate([cut[:, :, 0:2].reshape(rows, -1), cut[:, :, 2].reshape(rows, -1)], axis=1)
    total = jnp.concatenate([dot(normed_t, left), dot(cotangent_t, cut[:, :, 3].reshape(rows, -1))], axis=1)
    total = low(total).reshape(far, near, -1, groups * PACK)
    parts = [lax.dynamic_index_in_dim(total, here[0] ^ flip, 1, keepdims=False) for flip in range(near)]
    own = lax.axis_size("own")
    return [jnp.stack(parts[flip::own]) for flip in range(own)]


def gather_heads(parts, slot):
    first = lax.broadcasted_iota(jnp.int32, (1, HALF), 1) < HEAD
    base = slot // 2 * HALF
    pieces = []
    for even in range(0, len(parts), 2):
        left, right = parts[even][:, base : base + HALF], parts[even + 1][:, base : base + HALF]
        if slot % 2 == 0:
            right = pltpu.roll(right, HEAD, 1)
        else:
            left = pltpu.roll(left, HEAD, 1)
        pieces.append(jnp.where(first, left, right))
    return low(jnp.concatenate(pieces, axis=1))


def back_body(offset, heads, *refs):
    refs, (stacked, attended) = refs[:-2], refs[-2:]
    count = len(refs) - 4 if len(refs) < 12 else len(refs) - 11
    grads, refs = refs[:count], refs[count:]
    qkv_ref, out_ref = refs[:2]
    images_groups, tokens, _ = grads[0].shape
    groups = HEADS // heads
    images = images_groups // groups
    width = count * HEAD

    @pl.when(pl.program_id(0) == 0)
    def _():
        for image in range(images):
            rows = slice(image * tokens, (image + 1) * tokens)
            for group in range(groups):
                parts = [wide(ref[image * groups + group]) for ref in grads]
                attended[rows, group * width : (group + 1) * width] = gather_heads(parts, 3)
                for kind, slot in enumerate((2, 0, 1)):
                    start = (kind * groups + group) * width
                    stacked[rows, start : start + width] = gather_heads(parts, slot)

    starts = [group * heads * HEAD + offset * HEAD for group in range(groups)]
    inner = HEADS * HEAD
    weights = [qkv_ref[:, kind * inner + start :][:, :width] for kind in range(3) for start in starts]
    back = dot(stacked[...], jnp.concatenate(weights, axis=1), NT)
    mixed = dot(attended[...], jnp.concatenate([out_ref[start : start + width, :] for start in starts], axis=0))
    if len(refs) == 4:
        refs[2][...] = back
        refs[3][...] = mixed
        return
    back_in, mix_in, row_ref, mean_ref, inv_ref, gain_ref, back_ref, mix_ref, sum_ref = refs[2:]
    back = back + back_in[...]
    mixed = mixed + mix_in[...]
    back_ref[...] = back
    for image in range(images):
        rows = slice(image * tokens, (image + 1) * tokens)
        values = wide(row_ref[image])
        mix_ref[image] = low(values + mixed[rows])
        grad = back[rows] * gain_ref[...]
        centred = (values - mean_ref[image]) * inv_ref[image]
        sum_ref[0, image] = jnp.sum(grad, axis=0, keepdims=True)
        sum_ref[1, image] = jnp.sum(grad * centred, axis=0, keepdims=True)


def project_back(grads, full_qkv, full_out, heads, offset, images, tail=None):
    count = len(grads)
    groups = HEADS // heads
    tokens = grads[0].shape[1]
    channels, columns = full_qkv.shape
    step = 256 if channels % 256 == 0 else channels
    flat = (images * tokens, step)
    line = (images, 1, step)

    def across(shape):
        return pl.BlockSpec(shape, lambda n: (0,) * (len(shape) - 1) + (n,))

    in_specs = [pl.BlockSpec(grads[0].shape, lambda n: (0, 0, 0))] * count + [
        pl.BlockSpec((step, columns), lambda n: (n, 0)),
        across((HEADS * HEAD, step)),
    ]
    out_shape = [jax.ShapeDtypeStruct((images * tokens, channels), jnp.float32)]
    out_specs = [across(flat)]
    if tail is None:
        out_shape, out_specs = out_shape * 2, out_specs * 2
    else:
        rows = across((images, tokens, step))
        in_specs += [across(flat), across(flat), rows, across(line), across(line), across((1, step))]
        out_shape += [
            jax.ShapeDtypeStruct((images, tokens, channels), jnp.bfloat16),
            jax.ShapeDtypeStruct((2, images, 1, channels), jnp.float32),
        ]
        out_specs += [rows, across((2, *line))]
    return pl.pallas_call(
        functools.partial(back_body, offset, heads),
        out_shape=out_shape,
        grid=(channels // step,),
        in_specs=in_specs,
        out_specs=out_specs,
        scratch_shapes=[
            pltpu.VMEM((images * tokens, 3 * groups * count * HEAD), jnp.bfloat16),
            pltpu.VMEM((images * tokens, groups * count * HEAD), jnp.bfloat16),
        ],
        compiler_params=pltpu.CompilerParams(vmem_limit_bytes=VMEM),
        cost_estimate=pl.CostEstimate(
            flops=images * tokens * channels, bytes_accessed=2**12, transcendentals=0
        ),
        name="project_back",
    )(*grads, full_qkv, full_out, *(tail or ()))


def project_back_plain(grads, full_qkv, full_out, images):
    heads = len(grads)
    groups = HEADS // heads
    tokens = grads[0].shape[1]
    packed = jnp.stack(grads).reshape(heads, images, groups, tokens, 4, HEAD)
    packed = packed.transpose(1, 3, 4, 2, 0, 5).reshape(images, tokens, 4, HEADS * HEAD)
    key, value, query, attended = (packed[:, :, slot] for slot in range(4))
    stacked = jnp.concatenate([query, key, value], axis=2)
    mixed = jnp.einsum("itd,dc->itc", attended, full_out, preferred_element_type=jnp.float32)
    back = jnp.einsum("itd,cd->itc", stacked, full_qkv, preferred_element_type=jnp.float32)
    return mixed, back


def flipped(array, axis, flip):
    return lax.ppermute(array, axis, [(i, i ^ flip) for i in range(lax.axis_size(axis))])


def after(value, *others):
    return lax.optimization_barrier((value, others))[0]


def wide(array):
    return array.astype(jnp.float32)


def move_near(parts):
    rep = parts[0].shape[0]
    moved = []
    for own, part in enumerate(parts):
        for row in range(rep):
            flip = row * len(parts) + own
            moved.append(flipped(part[row], ("rep", "own"), flip) if flip else part[row])
    return moved


def sum_own(parts):
    total = wide(parts[0])
    for own in range(1, len(parts)):
        total = total + wide(flipped(parts[own], "own", own))
    return total


def sum_rep(total):
    mine = total[0]
    for row in range(1, total.shape[0]):
        mine = mine + wide(flipped(low(total[row]), "rep", row))
    return mine


def sum_half(near, groups):
    place = lax.axis_index("seq") % groups
    cut = near.reshape(2, groups, *near.shape[1:])
    total = lax.dynamic_index_in_dim(cut, place, 1, keepdims=False)
    for flip in range(1, groups):
        sent = lax.dynamic_index_in_dim(cut, place ^ flip, 1, keepdims=False)
        total = total + wide(flipped(low(sent), "seq", flip))
    return total


def sum_halves(total, groups):
    half = lax.axis_index("seq") // groups
    sent = lax.dynamic_index_in_dim(total, 1 - half, 0, keepdims=False)
    return lax.dynamic_index_in_dim(total, half, 0, keepdims=False) + wide(flipped(low(sent), "seq", groups))


def sum_seq(array, hold=()):
    bits = lax.axis_size("seq").bit_length() - 1
    for step in range(bits):
        if step == bits - 1:
            array = after(array, hold)
        bit = step - 1 if step else bits - 1
        array = array + flipped(array, "seq", 1 << bit)
    return array


def shards(latent, cotangent, norm_gain, norm_shift, proj_qkv, proj_out):
    tokens, images, channels = latent.shape
    seq_count = lax.axis_size("seq")
    devices = seq_count * lax.axis_size("rep") * lax.axis_size("own")
    per_group = channels // GROUPS
    total_count = tokens * seq_count * per_group
    groups = seq_count // images
    heads = HEADS // groups
    near = devices // seq_count
    block = channels // devices
    aligned = heads * HEAD % HALF == 0 and block % 8 == 0 and seq_count % 2 == 0
    here = (lax.axis_index("rep") * lax.axis_size("own") + lax.axis_index("own")).astype(jnp.int32).reshape(1)

    def weight_parts(grad):
        kernel = weight_grads if aligned else weight_grads_plain
        return kernel(normed_t, cotangent_t, grad, here, images, near, seq_count)

    full_qkv = lax.all_gather(proj_qkv, "own", axis=0, tiled=True)
    full_out = lax.all_gather(proj_out, "own", axis=0, tiled=True)

    def mean_groups(sums, hold=()):
        return sum_seq(sums.reshape(2, images, GROUPS, per_group).sum(axis=3), hold) / total_count

    def spread(array):
        return jnp.repeat(array, per_group, axis=1)[:, None, :]

    me = lax.axis_index("seq").astype(jnp.int32).reshape(1)
    unit = me % groups
    image = lax.axis_index("seq") // groups

    def pick(array, index):
        return lax.dynamic_index_in_dim(array, index, 0, keepdims=False)

    def swapped(array):
        return [pick(array, image), flipped(pick(array, 1 - image), "seq", groups)]

    rows = latent.transpose(1, 0, 2)
    cot_rows = cotangent.transpose(1, 0, 2)
    count = 2 if aligned else 1
    offsets = range(0, heads, count)
    grad_parts = []
    for offset in offsets:
        part = full_out.reshape(groups, heads, HEAD, channels)[:, offset : offset + count]
        part = part.reshape(groups * count * HEAD, channels)
        grad_parts.append(low(jnp.einsum("itc,dc->itd", cot_rows, part, preferred_element_type=jnp.float32)))
    work = swapped(rows)
    first_grad = grad_parts[0]

    values = rows.astype(jnp.float32)
    sums = jnp.stack([jnp.sum(values, axis=1), jnp.sum(values * values, axis=1)])
    group_mean, group_meansq = mean_groups(sums, first_grad)
    group_inv = lax.rsqrt(group_meansq - group_mean * group_mean + EPS)
    mean, inv_std = spread(group_mean), spread(group_inv)
    centred = (values - mean) * inv_std
    normed = low(centred * norm_gain + norm_shift)
    normed_t = normed.reshape(images * tokens, channels).T
    cotangent_t = cot_rows.reshape(images * tokens, channels).T
    work[1] = after(work[1], normed_t, cotangent_t)
    grad_parts[0] = swapped(after(grad_parts[0], work[1]))
    work_mean, work_inv = pick(mean, image), pick(inv_std, image)
    work = [low((wide(part) - work_mean) * work_inv * norm_gain + norm_shift) for part in work]

    def exchanged(pieces):
        return [pieces[0]] + [flipped(pieces[flip], "seq", flip) for flip in range(1, groups)]

    def grad_pieces(halves):
        pieces = []
        for flip in range(groups):
            start = (unit[0] ^ flip) * (count * HEAD)
            both = [lax.dynamic_slice_in_dim(half, start, count * HEAD, 1) for half in halves]
            pieces.append(jnp.pad(jnp.stack(both), ((0, 0), (0, 0), (0, HALF - count * HEAD))))
        return pieces

    arrays, heads_plan, moved = [], [], {}
    for index, offset in enumerate(offsets):
        base = len(arrays)
        if not aligned:
            arrays += project_plain(work, full_qkv, unit, heads, offset)
            heads_plan.append(((base, 0, 0), (base, HALF, 0), (base + 1, 0, 0)))
        elif index == 0:
            arrays += project(work, full_qkv, unit, heads, offset, (PACK, HALF))
            heads_plan.append(((base, 0, 0), (base, HALF, 0), (base + 2, 0, 0)))
            heads_plan.append(((base + 1, 0, 0), (base, HALF, 1), (base + 2, 0, 1)))
        else:
            arrays += project(work, full_qkv, unit, heads, offset, (PACK + HALF,))
            heads_plan.append(((base, 0, 0), (base, HALF, 0), (base + 1, 0, 0)))
            heads_plan.append(((base, PACK, 0), (base, HALF, 1), (base + 1, 0, 1)))
        if index:
            arrays.append(grad_parts[index])
        else:
            arrays.append(None)
    early = arrays[2 if aligned else 1 :][1:2]
    moved[0] = exchanged(arrays[0])
    first = 2 if aligned else 1
    arrays[first] = grad_pieces(after(grad_parts[0], moved[0], early))
    moved[first] = exchanged(arrays[first])
    for index in range(1, len(arrays)):
        if index != first:
            arrays[index] = after(arrays[index], moved[first])

    grads, nears = [], []
    result = None
    for head in range(heads):
        used = sorted({place[0] for place in heads_plan[head]})
        late = heads_plan[head][2][0]
        if late != first and late not in moved:
            halves = swapped(arrays[late])
            moved[late] = exchanged(grad_pieces(after(halves, first_result)))
        for index in used:
            if index not in moved:
                moved[index] = exchanged(arrays[index])
        operands = [moved[index] for index in used]
        if head >= 1:
            operands, result = lax.optimization_barrier((operands, result))
            grads.append(lax.all_to_all(result, "seq", split_axis=0, concat_axis=0, tiled=True))
        if head >= 2:
            operands = after(operands, grads[head - 2])
        if head == 2:
            parts = weight_parts(grads[0])
            operands = after(operands, parts)
            near_moved = move_near(parts)
        places = tuple((used.index(index), lane, half) for index, lane, half in heads_plan[head])
        result = attend_pair(operands, places, me)
        if head == 0:
            first_result = result
    if heads > 1:
        result = after(result, grads[-1])
    if heads > 2:
        result = after(result, near_moved)
        nears.append(sum(wide(part) for part in near_moved))
        grads[1:] = after(grads[1:], result)
    grads.append(lax.all_to_all(result, "seq", split_axis=0, concat_axis=0, tiled=True))
    back = mixed = jnp.zeros((images * tokens, channels), jnp.float32)
    if aligned and heads > count:
        back, mixed = project_back(grads[:count], full_qkv, full_out, heads, 0, images)
        grads[-1] = after(grads[-1], back, mixed)
    middle = [sum_own(weight_parts(grads[index])) for index in range(len(nears), heads - 1)]
    if middle:
        middle = [sum_rep(total) for total in middle]
        nears += middle
        grads[-1] = after(grads[-1], middle)
    last = sum_own(weight_parts(grads[-1]))
    if heads > 1:
        grads[-1], nears = after((grads[-1], nears), last)
    nears.append(sum_rep(last))
    gain = norm_gain[None, :]
    if aligned:
        offset = heads - count
        tail = (back, mixed, rows, mean, inv_std, gain)
        back, mixed_out, sums = project_back(grads[offset:], full_qkv, full_out, heads, offset, images, tail)
        back = back.reshape(images, tokens, channels)
        sums = sums.reshape(2, images, channels)
    else:
        mixed, back = project_back_plain(grads, full_qkv, full_out, images)
        mixed_out = low(values + mixed)
        sums = jnp.stack([jnp.sum(back * norm_gain, axis=1), jnp.sum(back * norm_gain * centred, axis=1)])
    sums = after(sums, nears[-1])
    weight_sums = []
    if heads > 1:
        early = sum_halves(sum_half(jnp.concatenate(nears[:-1], axis=2), groups), groups)
        weight_sums = jnp.split(early, heads - 1, axis=1)
    last_sum = sum_half(nears[-1], groups)
    weight_sums.append(sum_halves(last_sum, groups))

    mixed_out = after(mixed_out, last_sum).transpose(1, 0, 2)
    mean_one, mean_two = mean_groups(sums)
    grad_values = inv_std * (back * norm_gain - spread(mean_one) - centred * spread(mean_two))
    grad_latent = low(cot_rows.astype(jnp.float32) + grad_values).transpose(1, 0, 2)

    summed = jnp.stack(weight_sums)
    split = groups * HALF

    def columns(part):
        part = part.reshape(heads, block, groups, -1, HEAD).transpose(3, 1, 2, 0, 4)
        return part.reshape(-1, block, HEADS * HEAD)

    keys_values = columns(summed[:, :, :split])
    queries_outs = [columns(part)[0] for part in jnp.split(summed[:, :, split:], 2, axis=2)]
    grad_qkv = jnp.concatenate([queries_outs[0], keys_values[0], keys_values[1]], axis=1)
    out_rows = HEADS * HEAD // devices
    pieces = queries_outs[1].reshape(block, devices, out_rows).transpose(1, 2, 0)
    pieces = lax.all_to_all(pieces, ALL, split_axis=0, concat_axis=0, tiled=True)
    grad_out = pieces.transpose(1, 0, 2).reshape(out_rows, channels)
    return (mixed_out, grad_latent, grad_qkv, grad_out)


def solution(mesh):
    placed = (
        P("seq", ("rep", "own"), None),
        P("seq", ("rep", "own"), None),
        P(),
        P(),
        P("own", None),
        P("own", None),
    )
    return jax.shard_map(
        shards,
        mesh=mesh,
        in_specs=placed,
        out_specs=(
            P("seq", ("rep", "own"), None),
            P("seq", ("rep", "own"), None),
            P(ALL, None),
            P(ALL, None),
        ),
        check_vma=False,
    )
```
